512 devices in a mesh: seq: 64 (over y, z_lo, core), head: 8 (over z_hi, x).
Axes of the slice: x: 4, y: 8, z: 8 (z_hi: 2, z_lo: 4; z = z_hi * 4 + z_lo), core: 2. Of those that a mesh axis runs over, the one named last changes fastest.
Arguments:
- queries: bfloat16 [4096, 64, 576], P('seq', 'head'), may hold values from -17.5 to 17.5
- latents: bfloat16 [4096, 576], P('seq'), may hold values from -6 to 6
- positions: int32 [4096], P('seq'), may hold values from 0 to 4095, as said below
- lengths: int32 [8], replicated, may hold values from 1 to 1024, 4096 in all
- value_up: bfloat16 [64, 512, 128], P('head'), may hold values from -1 to 1
- out_weight: bfloat16 [8192, 4096], P('head', 'seq'), may hold values from -0.0625 to 0.0625
Outputs:
- mixed: bfloat16 [4096, 4096], P('seq', 'head')
The draws below stay inside these ranges and needn't reach their ends.
Inputs may be any that keep to these rules, and one draw needn't show every extreme that they name: A permutation: stored token r sits at sequence position positions[r]. `lengths`: segment 0 is the problem statement, the others are solutions; they sum to 4096.
All inputs are finite; a program needn't handle non-finite values.
Results may differ from the reference program's by a relative error of at most 0.022.
Values may be sent and summed in bfloat16 or wider, within the bound.
No kernel may reach another device: no remote copies, remote signals or barrier semaphores. Data moves between devices by JAX's collectives and lax.ppermute only.
A program may use at most 64 MiB of HBM per device.

```python
import math
import jax
import jax.numpy as jnp
import numpy as np
from jax import lax

TOK_DEV = 64
HEADS = 64
LATENT = 512
ROPE = 64
VH = 128
D_OUT = 4096
NSEG = 8
TOKENS = 4096


def shared_order(key):
    return jax.random.permutation(jax.random.fold_in(key, 7), TOKENS).astype(jnp.int32)


def draw_positions(key, part):
    return shared_order(key)


def draw_latents(key, part):
    key = jax.random.fold_in(key, 5)
    drawn = jax.random.normal(key, (TOKENS, LATENT + ROPE), jnp.float32)
    return jnp.clip(drawn, -6.0, 6.0).astype(jnp.bfloat16)


def draw_queries(key, part):
    key = jax.random.fold_in(key, 9)
    drawn = jax.random.normal(key, (TOKENS, HEADS, LATENT + ROPE), jnp.float32)
    return jnp.clip(drawn, -6.0, 6.0).astype(jnp.bfloat16)


def shard_levels(key, extent, pieces, low, largest):
    factor_of = 1.0
    for axis_at, shards_of in pieces:
        steps = jax.random.uniform(jax.random.fold_in(jax.random.fold_in(key, 6), axis_at), (shards_of,), jnp.float32, low / len(pieces), largest / len(pieces))
        factor_of = factor_of * jnp.repeat(jnp.exp(steps), extent[axis_at] // shards_of).reshape((-1,) + (1,) * (len(extent) - 1 - axis_at))
    return factor_of


def profile(amount, total, reach, slope):
    weights = [(1 << 20) // math.isqrt(rank ** slope) + 1 for rank in range(2, amount + 1)]
    spare, given = total - reach - (amount - 1), [1] * (amount - 1)
    while spare > 0:
        movable = [i for i in range(amount - 1) if given[i] < reach]
        mass, remaining = sum([weights[i] for i in movable]), spare
        for i in movable:
            extra = min(reach - given[i], max(1, remaining * weights[i] // mass), spare)
            given[i] = given[i] + extra
            spare = spare - extra
    return np.array([reach] + given)


def ragged(stream_key, number_of, total, reach, lean):
    if number_of == 2:
        one = jax.random.randint(stream_key, (), max(1, total - reach), min(reach, total - 1) + 1)
        return jnp.stack([one, total - one])
    sizes = jnp.asarray(profile(number_of, total, reach, lean), jnp.int32)
    couples = (number_of - 1) // 2
    source_of, receiver = sizes[1:1 + 2 * couples:2], sizes[2:2 + 2 * couples:2]
    slack = jnp.minimum(source_of - 1, reach - receiver)
    shifted = jax.random.randint(jax.random.fold_in(stream_key, 1), (couples,), 0, 1 << 20) % (slack + 1)
    sizes = sizes.at[1:1 + 2 * couples:2].set(source_of - shifted).at[2:2 + 2 * couples:2].set(receiver + shifted)
    return sizes[jax.random.permutation(jax.random.fold_in(stream_key, 2), number_of)]


def scatter_about(key, extent, scale, reach, split=(), held_as=jnp.bfloat16):
    result = scale * jax.random.normal(key, extent, jnp.float32)
    if split:
        result = result * shard_levels(key, extent, split, -0.22, 0.18)
    return jnp.clip(result, -reach, reach).astype(held_as)


def setup_inputs(seed: int = 0) -> dict:
    keys = jax.random.split(jax.random.key(seed), 7)
    queries = draw_queries(jax.random.fold_in(keys[6], 71), 0)
    latents = draw_latents(jax.random.fold_in(keys[6], 71), 0)
    positions = draw_positions(jax.random.fold_in(keys[6], 71), 0)
    lengths = ragged(keys[3], NSEG, TOKENS, TOKENS // 4, 2).astype(jnp.int32)
    value_up = scatter_about(keys[4], (HEADS, LATENT, VH), (LATENT // 16) ** -0.5, 1.0, ((0, 8),))
    out_weight = scatter_about(keys[5], (HEADS * VH, D_OUT), (HEADS * VH) ** -0.5, 0.0625, ((0, 8), (1, 64)))
    return dict(queries=queries, latents=latents, positions=positions, lengths=lengths, value_up=value_up, out_weight=out_weight)


SCALE = 192.0 ** -0.5


def segment_of(where, lengths):
    segment_ends = jnp.cumsum(lengths).astype(jnp.int32)
    return jnp.sum((where[:, None] >= segment_ends[None, :]).astype(jnp.int32), axis=1).astype(jnp.int32)


def apply_rope(rotary, where):
    full_width = rotary.shape[-1]
    half_width = full_width // 2
    frequency = jnp.exp(jnp.arange(half_width, dtype=jnp.float32) * (-2.0 * math.log(10000.0) / full_width))
    angles = where.astype(jnp.float32)[:, None] * frequency[None, :]
    target_shape = (angles.shape[0],) + (1,) * (rotary.ndim - 2) + (half_width,)
    cosines = jnp.cos(angles).reshape(target_shape)
    sines = jnp.sin(angles).reshape(target_shape)
    first_half = rotary[..., :half_width].astype(jnp.float32)
    second_half = rotary[..., half_width:].astype(jnp.float32)
    return jnp.concatenate([first_half * cosines - second_half * sines, first_half * sines + second_half * cosines], axis=-1)


def prepare(source, where):
    turned = apply_rope(source[..., LATENT:], where)
    return jnp.concatenate([source[..., :LATENT].astype(jnp.float32), turned], axis=-1).astype(jnp.bfloat16)


def reference(queries, latents, positions, lengths, value_up, out_weight):
    q_rot = prepare(queries, positions)
    k_rot = prepare(latents, positions)
    segment = segment_of(positions, lengths)
    keys_full = k_rot.astype(jnp.float32)
    values_full = k_rot[:, :LATENT].astype(jnp.float32)
    up_full = value_up.astype(jnp.float32)
    starts = jnp.arange(TOKENS // TOK_DEV, dtype=jnp.int32) * TOK_DEV

    def one_block(offset):
        query_block = lax.dynamic_slice_in_dim(q_rot, offset, TOK_DEV, 0).astype(jnp.float32)
        query_pos = lax.dynamic_slice_in_dim(positions, offset, TOK_DEV, 0)
        query_seg = lax.dynamic_slice_in_dim(segment, offset, TOK_DEV, 0)
        scores = jnp.einsum('thw,kw->thk', query_block, keys_full) * SCALE
        visible = (positions[None, :] <= query_pos[:, None]) & ((segment[None, :] == query_seg[:, None]) | (segment[None, :] == 0))
        visible = visible[:, None, :]
        row_max = jnp.max(jnp.where(visible, scores, -1e30), axis=-1)
        weights = jnp.where(visible, jnp.exp(scores - row_max[..., None]), 0.0)
        totals = jnp.sum(weights, axis=-1)
        probs = weights.astype(jnp.bfloat16)
        context = (jnp.einsum('thk,kl->thl', probs.astype(jnp.float32), values_full) / totals[..., None]).astype(jnp.bfloat16)
        values = jnp.einsum('thl,hlv->thv', context.astype(jnp.float32), up_full).astype(jnp.bfloat16)
        return values.reshape(TOK_DEV, HEADS * VH)

    values = lax.map(one_block, starts).reshape(TOKENS, HEADS * VH)
    return jnp.dot(values, out_weight, preferred_element_type=jnp.float32).astype(jnp.bfloat16)
```

```python
import functools
import math

import jax
import jax.numpy as jnp
import numpy as np
from jax import lax
from jax.experimental import pallas as pl
from jax.experimental.pallas import tpu as pltpu
from jax.sharding import Mesh, PartitionSpec as P

LATENT = 512
ROPE = 64
WIDTH = 640
SCALE = 192.0 ** (-0.5)
LOG2_SCALE = SCALE * math.log2(math.e)
HIDDEN = -1e30
VMEM = 48 * 1024 * 1024
NT = (((1,), (1,)), ((), ()))


def rotate(rotary, where):
    half = ROPE // 2
    frequency = jnp.exp(jnp.arange(half, dtype=jnp.float32) * (-2.0 * math.log(10000.0) / ROPE))
    angles = where.astype(jnp.float32)[:, None] * frequency[None, :]
    shape = (angles.shape[0],) + (1,) * (rotary.ndim - 2) + (half,)
    cosines = jnp.cos(angles).reshape(shape)
    sines = jnp.sin(angles).reshape(shape)
    first = rotary[..., :half].astype(jnp.float32)
    second = rotary[..., half:].astype(jnp.float32)
    return jnp.concatenate(
        [first * cosines - second * sines, first * sines + second * cosines], axis=-1
    ).astype(jnp.bfloat16)


def position_parts(where):
    return jnp.stack([where >> 6, where & 63], axis=-1).astype(jnp.bfloat16)


def shift_z(x, by):
    perm = []
    for z in range(8):
        to = (z + by) % 8
        source = ((z % 4) // 2 * 2 + z % 2) * 2 + z // 4
        target = ((to % 4) // 2 * 2 + to % 2) * 2 + to // 4
        perm.append((source, target))
    return lax.ppermute(x, ("zh_lat", "zl_lat", "z_hi"), perm)


def swap(x, axis):
    return lax.ppermute(x, axis, [(0, 1), (1, 0)])


def attend_kernel(blocks, first, last, *refs):
    ends_ref, q_ref = refs[0], refs[1]
    key_refs = refs[2 : 2 + blocks]
    rest = refs[2 + blocks :]
    if not first:
        m_in, l_in, acc_in = rest[:3]
        rest = rest[3:]
    if last:
        up_ref, out_ref = rest
    else:
        m_out, l_out, acc_out = rest
    heads, toks, _ = q_ref.shape
    rows = heads * toks
    meta = q_ref[0, :, LATENT:].astype(jnp.float32)
    query_pos = meta[:, 66:67] * 64.0 + meta[:, 67:68]
    query_start = jnp.zeros_like(query_pos)
    for k in range(8):
        end = ends_ref[k].astype(jnp.float32)
        query_start = jnp.where(query_pos >= end, end, query_start)
    first_end = ends_ref[0].astype(jnp.float32)
    q = q_ref[...].reshape(rows, WIDTH)
    lane = lax.broadcasted_iota(jnp.int32, (toks, 128), 1)
    pick = jnp.where(lane == 64, 64.0, jnp.where(lane == 65, 1.0, 0.0)).astype(jnp.bfloat16)
    scores = []
    for key_ref in key_refs:
        keys = key_ref[...]
        key_pos = lax.dot_general(
            pick, keys[:, LATENT:], NT, preferred_element_type=jnp.float32
        )
        visible = (key_pos <= query_pos) & ((key_pos >= query_start) | (key_pos < first_end))
        raw = lax.dot_general(q, keys, NT, preferred_element_type=jnp.float32)
        raw = raw.reshape(heads, toks, keys.shape[0])
        scores.append(jnp.where(visible[None], raw, HIDDEN).reshape(rows, keys.shape[0]))
    top = functools.reduce(jnp.maximum, [jnp.max(s, axis=1, keepdims=True) for s in scores])
    if not first:
        old = m_in[...].reshape(rows, 128)[:, :1]
        top = jnp.maximum(top, old)
        fade = jnp.exp2((old - top) * LOG2_SCALE)
    total = 0.0
    mixed = 0.0
    for key_ref, s in zip(key_refs, scores):
        weights = jnp.exp2((s - top) * LOG2_SCALE)
        total = total + jnp.sum(weights, axis=1, keepdims=True)
        mixed = mixed + jnp.dot(
            weights.astype(jnp.bfloat16), key_ref[:, :LATENT], preferred_element_type=jnp.float32
        )
    if not first:
        total = total + fade * l_in[...].reshape(rows, 128)[:, :1]
        mixed = mixed + fade * acc_in[...].reshape(rows, LATENT)
    if not last:
        m_out[...] = jnp.broadcast_to(top, (rows, 128)).reshape(heads, toks, 128)
        l_out[...] = jnp.broadcast_to(total, (rows, 128)).reshape(heads, toks, 128)
        acc_out[...] = mixed.reshape(heads, toks, LATENT)
        return
    context = (mixed / total).astype(jnp.bfloat16).reshape(heads, toks, LATENT)
    level = (top * LOG2_SCALE + jnp.log2(total)).reshape(heads, toks, 1)
    half = toks // 2
    for h in range(heads):
        part = jnp.dot(context[h], up_ref[h], preferred_element_type=jnp.float32)
        at = slice(h * 128, h * 128 + 128)
        spread = jnp.broadcast_to(level[h], (toks, 128))
        for side in range(2):
            out_ref[side, 0, :, at] = part[side * half : (side + 1) * half]
            out_ref[side, 1, :, at] = spread[side * half : (side + 1) * half]


def attend(ends, q, keys, carry=None, up=None, group=2):
    heads, toks, _ = q.shape
    first, last = carry is None, up is not None
    per_head = lambda width: pl.BlockSpec((group, toks, width), lambda i: (i, 0, 0))
    in_specs = [pl.BlockSpec(memory_space=pltpu.SMEM), per_head(WIDTH)]
    in_specs += [pl.BlockSpec(k.shape, lambda i: (0, 0)) for k in keys]
    args = [ends, q, *keys]
    state_specs = [per_head(128), per_head(128), per_head(LATENT)]
    if not first:
        in_specs += state_specs
        args += list(carry)
    if last:
        in_specs.append(pl.BlockSpec((group, LATENT, 128), lambda i: (i, 0, 0)))
        args.append(up)
        out_shape = jax.ShapeDtypeStruct((2, 2, toks // 2, heads * 128), jnp.float32)
        out_specs = pl.BlockSpec((2, 2, toks // 2, group * 128), lambda i: (0, 0, 0, i))
    else:
        out_shape = [
            jax.ShapeDtypeStruct((heads, toks, w), jnp.float32) for w in (128, 128, LATENT)
        ]
        out_specs = state_specs
    count = sum(k.shape[0] for k in keys)
    rows = heads * toks
    return pl.pallas_call(
        functools.partial(attend_kernel, len(keys), first, last),
        grid=(heads // group,),
        in_specs=in_specs,
        out_specs=out_specs,
        out_shape=out_shape,
        compiler_params=pltpu.CompilerParams(vmem_limit_bytes=VMEM),
        cost_estimate=pl.CostEstimate(
            flops=2 * rows * count * (WIDTH + LATENT),
            bytes_accessed=2 * count * WIDTH + rows * 4096,
            transcendentals=rows * count,
        ),
    )(*args)


def project_kernel(here_ref, v_ref, own_ref, other_ref, out_ref):
    core, near = here_ref[0], here_ref[1]
    half = v_ref.shape[1] // 2
    v_own = v_ref[:, pl.ds(pl.multiple_of(core * half, half), half)]
    v_other = v_ref[:, pl.ds(pl.multiple_of((1 - core) * half, half), half)]
    part = lax.dot_general(v_own, own_ref[0], NT, preferred_element_type=jnp.float32)
    part += lax.dot_general(v_other, other_ref[0], NT, preferred_element_type=jnp.float32)
    toks = part.shape[0] // 2
    part = part.astype(jnp.bfloat16)
    out_ref[0, near] = part[:toks]
    out_ref[0, 1 - near] = part[toks:]


def project(here, v, w_own, w_other):
    blocks, cols, depth = w_own.shape
    toks = v.shape[0] // 2
    return pl.pallas_call(
        project_kernel,
        grid=(blocks,),
        in_specs=[
            pl.BlockSpec(memory_space=pltpu.SMEM),
            pl.BlockSpec(v.shape, lambda i: (0, 0)),
            pl.BlockSpec((1, cols, depth), lambda i: (i, 0, 0)),
            pl.BlockSpec((1, cols, depth), lambda i: (i, 0, 0)),
        ],
        out_specs=pl.BlockSpec((1, 2, toks, cols), lambda i: (i, 0, 0, 0)),
        out_shape=jax.ShapeDtypeStruct((blocks, 2, toks, cols), jnp.bfloat16),
        compiler_params=pltpu.CompilerParams(vmem_limit_bytes=VMEM),
        cost_estimate=pl.CostEstimate(
            flops=8 * toks * blocks * cols * depth,
            bytes_accessed=4 * blocks * cols * depth,
            transcendentals=0,
        ),
    )(here, v, w_own, w_other)


def total_kernel(parts_ref, out_ref):
    heads = parts_ref.shape[0]
    for near in range(2):
        total = parts_ref[0, near].astype(jnp.float32)
        for h in range(1, heads):
            total += parts_ref[h, near].astype(jnp.float32)
        for far in range(2):
            at = far * 256 + near * 128
            out_ref[:, at : at + 128] = total[:, far * 128 : far * 128 + 128].astype(out_ref.dtype)


def add_heads(parts):
    _, _, toks, cols = parts.shape
    return pl.pallas_call(
        total_kernel,
        out_shape=jax.ShapeDtypeStruct((toks, 2 * cols), jnp.bfloat16),
        compiler_params=pltpu.CompilerParams(vmem_limit_bytes=VMEM),
    )(parts)


def on_device(queries, latents, positions, lengths, value_up, out_weight):
    toks, heads, width = queries.shape
    ends = jnp.cumsum(lengths).astype(jnp.int32)
    core = lax.axis_index("core").astype(jnp.int32)
    far = lax.axis_index("zh_lat")
    near = lax.axis_index("zl_lat").astype(jnp.int32)

    parts = position_parts(positions)
    zeros = lambda n: jnp.zeros((toks, n), jnp.bfloat16)
    key_rows = jnp.concatenate(
        [latents[:, :LATENT], rotate(latents[:, LATENT:], positions), parts, zeros(62)], axis=1
    )
    along_y = lax.all_to_all(
        jnp.broadcast_to(key_rows[None], (8, toks, WIDTH)), "y", 0, 0
    ).reshape(8 * toks, WIDTH)

    tail = jnp.concatenate([zeros(2), parts, zeros(60)], axis=1)
    q_own = jnp.concatenate(
        [
            queries[..., :LATENT],
            rotate(queries[..., LATENT:], positions),
            jnp.broadcast_to(tail[:, None, :], (toks, heads, 64)),
        ],
        axis=2,
    ).transpose(1, 0, 2)
    q = jnp.concatenate([q_own, swap(q_own, "core")], axis=1)

    from_left = shift_z(along_y, 1)
    from_right = shift_z(along_y, -1)
    carry = attend(ends, q, [along_y])
    middle = along_y.shape[0] // 2
    across_left = shift_z(from_left[:middle], 1)
    across_right = shift_z(from_right[middle:], -1)
    carry = attend(ends, q, [from_left, from_right], carry)

    w, _ = lax.optimization_barrier((out_weight.T, along_y))
    w = lax.all_to_all(w, "core", 1, 0, tiled=True)
    w_far = swap(w, "zh_lat")
    w = jnp.where(far == 0, jnp.stack([w, w_far]), jnp.stack([w_far, w]))
    w_own = lax.all_gather(w.reshape(1, -1, w.shape[2]), "y", axis=0, tiled=True)
    w_other = swap(w_own, "core")

    both = attend(ends, q, [across_left, across_right], carry, value_up)
    mine, theirs = both[0], swap(both[1], "core")
    level = jnp.maximum(mine[1], theirs[1])
    share_mine = jnp.exp2(mine[1] - level)
    share_theirs = jnp.exp2(theirs[1] - level)
    values = (
        (mine[0] * share_mine + theirs[0] * share_theirs) / (share_mine + share_theirs)
    ).astype(jnp.bfloat16)
    v = jnp.concatenate([values, swap(values, "zl_lat")], axis=0)

    partial = project(jnp.stack([core, near]), v, w_own, w_other)
    rows = partial.shape[2]
    cols = partial.shape[3]
    arrived = lax.all_to_all(
        partial.reshape(16, rows, cols), ("z_hi", "x", "zl_lat"), 0, 0
    ).reshape(8, 2, rows, cols)
    return add_heads(arrived)


def solution(mesh):
    grid = Mesh(
        mesh.devices.reshape(8, 2, 2, 2, 2, 4), ("y", "zh_lat", "zl_lat", "core", "z_hi", "x")
    )
    seq, head = ("y", "zh_lat", "zl_lat", "core"), ("z_hi", "x")
    placed = (
        P(seq, head, None),
        P(seq, None),
        P(seq),
        P(),
        P(head, None, None),
        P(head, seq),
    )
    return jax.shard_map(
        on_device, mesh=grid, in_specs=placed, out_specs=P(seq, head), check_vma=False
    )
```

```python
import functools
import math

import jax
import jax.numpy as jnp
import numpy as np
from jax import lax
from jax.experimental import pallas as pl
from jax.experimental.pallas import tpu as pltpu
from jax.sharding import Mesh, PartitionSpec as P

LATENT = 512
ROPE = 64
WIDTH = 640
SCALE = 192.0 ** (-0.5)
LOG2_SCALE = SCALE * math.log2(math.e)
HIDDEN = -1e30
VMEM = 48 * 1024 * 1024
NT = (((1,), (1,)), ((), ()))


def rotate(rotary, where):
    half = ROPE // 2
    frequency = jnp.exp(jnp.arange(half, dtype=jnp.float32) * (-2.0 * math.log(10000.0) / ROPE))
    angles = where.astype(jnp.float32)[:, None] * frequency[None, :]
    shape = (angles.shape[0],) + (1,) * (rotary.ndim - 2) + (half,)
    cosines = jnp.cos(angles).reshape(shape)
    sines = jnp.sin(angles).reshape(shape)
    first = rotary[..., :half].astype(jnp.float32)
    second = rotary[..., half:].astype(jnp.float32)
    return jnp.concatenate(
        [first * cosines - second * sines, first * sines + second * cosines], axis=-1
    ).astype(jnp.bfloat16)


def position_parts(where):
    return jnp.stack([where >> 6, where & 63], axis=-1).astype(jnp.bfloat16)


def shift_z(x, by):
    perm = []
    for z in range(8):
        to = (z + by) % 8
        source = ((z % 4) // 2 * 2 + z % 2) * 2 + z // 4
        target = ((to % 4) // 2 * 2 + to % 2) * 2 + to // 4
        perm.append((source, target))
    return lax.ppermute(x, ("zh_lat", "zl_lat", "z_hi"), perm)


def swap(x, axis):
    return lax.ppermute(x, axis, [(0, 1), (1, 0)])


def attend_kernel(blocks, first, last, *refs):
    ends_ref, q_ref = refs[0], refs[1]
    key_refs = refs[2 : 2 + blocks]
    rest = refs[2 + blocks :]
    if not first:
        m_in, l_in, acc_in = rest[:3]
        rest = rest[3:]
    if last:
        up_ref, out_ref = rest
    else:
        m_out, l_out, acc_out = rest
    heads, toks, _ = q_ref.shape
    rows = heads * toks
    meta = q_ref[0, :, LATENT:].astype(jnp.float32)
    query_pos = meta[:, 66:67] * 64.0 + meta[:, 67:68]
    query_start = jnp.zeros_like(query_pos)
    for k in range(8):
        end = ends_ref[k].astype(jnp.float32)
        query_start = jnp.where(query_pos >= end, end, query_start)
    first_end = ends_ref[0].astype(jnp.float32)
    q = q_ref[...].reshape(rows, WIDTH)
    lane = lax.broadcasted_iota(jnp.int32, (toks, 128), 1)
    pick = jnp.where(lane == 64, 64.0, jnp.where(lane == 65, 1.0, 0.0)).astype(jnp.bfloat16)
    scores = []
    for key_ref in key_refs:
        keys = key_ref[...]
        key_pos = lax.dot_general(
            pick, keys[:, LATENT:], NT, preferred_element_type=jnp.float32
        )
        visible = (key_pos <= query_pos) & ((key_pos >= query_start) | (key_pos < first_end))
        raw = lax.dot_general(q, keys, NT, preferred_element_type=jnp.float32)
        raw = raw.reshape(heads, toks, keys.shape[0])
        scores.append(jnp.where(visible[None], raw, HIDDEN).reshape(rows, keys.shape[0]))
    top = functools.reduce(jnp.maximum, [jnp.max(s, axis=1, keepdims=True) for s in scores])
    if not first:
        old = m_in[...].reshape(rows, 128)[:, :1]
        top = jnp.maximum(top, old)
        fade = jnp.exp2((old - top) * LOG2_SCALE)
    total = 0.0
    mixed = 0.0
    for key_ref, s in zip(key_refs, scores):
        weights = jnp.exp2((s - top) * LOG2_SCALE)
        total = total + jnp.sum(weights, axis=1, keepdims=True)
        mixed = mixed + jnp.dot(
            weights.astype(jnp.bfloat16), key_ref[:, :LATENT], preferred_element_type=jnp.float32
        )
    if not first:
        total = total + fade * l_in[...].reshape(rows, 128)[:, :1]
        mixed = mixed + fade * acc_in[...].reshape(rows, LATENT)
    if not last:
        m_out[...] = jnp.broadcast_to(top, (rows, 128)).reshape(heads, toks, 128)
        l_out[...] = jnp.broadcast_to(total, (rows, 128)).reshape(heads, toks, 128)
        acc_out[...] = mixed.reshape(heads, toks, LATENT)
        return
    context = (mixed / total).astype(jnp.bfloat16).reshape(heads, toks, LATENT)
    level = (top * LOG2_SCALE + jnp.log2(total)).reshape(heads, toks, 1)
    half = toks // 2
    for h in range(heads):
        part = jnp.dot(context[h], up_ref[h], preferred_element_type=jnp.float32)
        at = slice(h * 128, h * 128 + 128)
        spread = jnp.broadcast_to(level[h], (toks, 128))
        for side in range(2):
            out_ref[side, 0, :, at] = part[side * half : (side + 1) * half]
            out_ref[side, 1, :, at] = spread[side * half : (side + 1) * half]


def attend(ends, q, keys, carry=None, up=None, group=2):
    heads, toks, _ = q.shape
    first, last = carry is None, up is not None
    per_head = lambda width: pl.BlockSpec((group, toks, width), lambda i: (i, 0, 0))
    in_specs = [pl.BlockSpec(memory_space=pltpu.SMEM), per_head(WIDTH)]
    in_specs += [pl.BlockSpec(k.shape, lambda i: (0, 0)) for k in keys]
    args = [ends, q, *keys]
    state_specs = [per_head(128), per_head(128), per_head(LATENT)]
    if not first:
        in_specs += state_specs
        args += list(carry)
    if last:
        in_specs.append(pl.BlockSpec((group, LATENT, 128), lambda i: (i, 0, 0)))
        args.append(up)
        out_shape = jax.ShapeDtypeStruct((2, 2, toks // 2, heads * 128), jnp.float32)
        out_specs = pl.BlockSpec((2, 2, toks // 2, group * 128), lambda i: (0, 0, 0, i))
    else:
        out_shape = [
            jax.ShapeDtypeStruct((heads, toks, w), jnp.float32) for w in (128, 128, LATENT)
        ]
        out_specs = state_specs
    count = sum(k.shape[0] for k in keys)
    rows = heads * toks
    return pl.pallas_call(
        functools.partial(attend_kernel, len(keys), first, last),
        grid=(heads // group,),
        in_specs=in_specs,
        out_specs=out_specs,
        out_shape=out_shape,
        compiler_params=pltpu.CompilerParams(vmem_limit_bytes=VMEM),
        cost_estimate=pl.CostEstimate(
            flops=2 * rows * count * (WIDTH + LATENT),
            bytes_accessed=2 * count * WIDTH + rows * 4096,
            transcendentals=rows * count,
        ),
    )(*args)


def project_kernel(near_ref, v_ref, w_ref, out_ref):
    near = near_ref[0]
    part = lax.dot_general(v_ref[...], w_ref[0], NT, preferred_element_type=jnp.float32)
    toks = part.shape[0] // 2
    part = part.astype(jnp.bfloat16)
    out_ref[0, near] = part[:toks]
    out_ref[0, 1 - near] = part[toks:]


def project(near, v, w):
    blocks, cols, depth = w.shape
    toks = v.shape[0] // 2
    return pl.pallas_call(
        project_kernel,
        grid=(blocks,),
        in_specs=[
            pl.BlockSpec(memory_space=pltpu.SMEM),
            pl.BlockSpec(v.shape, lambda i: (0, 0)),
            pl.BlockSpec((1, cols, depth), lambda i: (i, 0, 0)),
        ],
        out_specs=pl.BlockSpec((1, 2, toks, cols), lambda i: (i, 0, 0, 0)),
        out_shape=jax.ShapeDtypeStruct((blocks, 2, toks, cols), jnp.bfloat16),
        compiler_params=pltpu.CompilerParams(vmem_limit_bytes=VMEM),
        cost_estimate=pl.CostEstimate(
            flops=4 * toks * blocks * cols * depth,
            bytes_accessed=2 * blocks * cols * depth,
            transcendentals=0,
        ),
    )(near, v, w)


def total_kernel(parts_ref, out_ref):
    heads = parts_ref.shape[0]
    for near in range(2):
        total = parts_ref[0, near].astype(jnp.float32)
        for h in range(1, heads):
            total += parts_ref[h, near].astype(jnp.float32)
        for far in range(2):
            at = far * 256 + near * 128
            out_ref[:, at : at + 128] = total[:, far * 128 : far * 128 + 128].astype(out_ref.dtype)


def add_heads(parts):
    _, _, toks, cols = parts.shape
    return pl.pallas_call(
        total_kernel,
        out_shape=jax.ShapeDtypeStruct((toks, 2 * cols), jnp.bfloat16),
        compiler_params=pltpu.CompilerParams(vmem_limit_bytes=VMEM),
    )(parts)


def on_device(queries, latents, positions, lengths, value_up, out_weight):
    toks, heads, width = queries.shape
    ends = jnp.cumsum(lengths).astype(jnp.int32)
    near = lax.axis_index("zl_lat").astype(jnp.int32)

    w = lax.all_gather(out_weight.T, ("y", "zh_lat", "core"), axis=0, tiled=True)
    w = w.reshape(8, w.shape[0] // 8, w.shape[1])

    parts = position_parts(positions)
    zeros = lambda n: jnp.zeros((toks, n), jnp.bfloat16)
    key_rows = jnp.concatenate(
        [latents[:, :LATENT], rotate(latents[:, LATENT:], positions), parts, zeros(62)], axis=1
    )
    along_y = lax.all_to_all(
        jnp.broadcast_to(key_rows[None], (8, toks, WIDTH)), "y", 0, 0
    ).reshape(8 * toks, WIDTH)

    tail = jnp.concatenate([zeros(2), parts, zeros(60)], axis=1)
    q_own = jnp.concatenate(
        [
            queries[..., :LATENT],
            rotate(queries[..., LATENT:], positions),
            jnp.broadcast_to(tail[:, None, :], (toks, heads, 64)),
        ],
        axis=2,
    ).transpose(1, 0, 2)
    q = jnp.concatenate([q_own, swap(q_own, "core")], axis=1)

    from_left = shift_z(along_y, 1)
    from_right = shift_z(along_y, -1)
    carry = attend(ends, q, [along_y], group=8)
    middle = along_y.shape[0] // 2
    across_left = shift_z(from_left[:middle], 1)
    across_right = shift_z(from_right[middle:], -1)
    carry = attend(ends, q, [from_left, from_right], carry, group=8)

    both = attend(ends, q, [across_left, across_right], carry, value_up)
    mine, theirs = both[0], swap(both[1], "core")
    level = jnp.maximum(mine[1], theirs[1])
    share_mine = jnp.exp2(mine[1] - level)
    share_theirs = jnp.exp2(theirs[1] - level)
    values = (
        (mine[0] * share_mine + theirs[0] * share_theirs) / (share_mine + share_theirs)
    ).astype(jnp.bfloat16)
    v = jnp.concatenate([values, swap(values, "zl_lat")], axis=0)

    partial = project(near.reshape(1), v, w)
    rows = partial.shape[2]
    cols = partial.shape[3]
    arrived = lax.all_to_all(
        partial.reshape(16, rows, cols), ("z_hi", "x", "zl_lat"), 0, 0
    ).reshape(8, 2, rows, cols)
    return add_heads(arrived)


def solution(mesh):
    grid = Mesh(
        mesh.devices.reshape(8, 2, 2, 2, 2, 4), ("y", "zh_lat", "zl_lat", "core", "z_hi", "x")
    )
    seq, head = ("y", "zh_lat", "zl_lat", "core"), ("z_hi", "x")
    placed = (
        P(seq, head, None),
        P(seq, None),
        P(seq),
        P(),
        P(head, None, None),
        P(head, seq),
    )
    return jax.shard_map(
        on_device, mesh=grid, in_specs=placed, out_specs=P(seq, head), check_vma=False
    )
```

```python
import functools
import math

import jax
import jax.numpy as jnp
import numpy as np
from jax import lax
from jax.experimental import pallas as pl
from jax.experimental.pallas import tpu as pltpu
from jax.sharding import Mesh, PartitionSpec as P

LATENT = 512
ROPE = 64
WIDTH = 640
SCALE = 192.0 ** (-0.5)
LOG2_SCALE = SCALE * math.log2(math.e)
HIDDEN = -1e30
VMEM = 48 * 1024 * 1024
NT = (((1,), (1,)), ((), ()))


def turns(where_ref, frequency_ref):
    toks = where_ref.shape[1]
    row = lax.broadcasted_iota(jnp.int32, (toks, toks), 0)
    column = lax.broadcasted_iota(jnp.int32, (toks, toks), 1)
    spread = jnp.broadcast_to(where_ref[...], (toks, toks))
    where = jnp.sum(jnp.where(row == column, spread, 0).astype(jnp.float32), axis=1, keepdims=True)
    angles = where * frequency_ref[...]
    sines = jnp.sin(angles)
    lane = lax.broadcasted_iota(jnp.int32, sines.shape, 1)
    return where, jnp.cos(angles), jnp.where(lane < ROPE // 2, -sines, sines)


def turned(rotary, cosines, sines):
    half = ROPE // 2
    other = jnp.concatenate([rotary[:, half:], rotary[:, :half]], axis=1)
    return rotary * cosines + other * sines


def position_parts(where):
    high = jnp.floor(where * (1.0 / 64.0))
    return high, where - 64.0 * high


def key_kernel(where_ref, frequency_ref, latents_ref, out_ref):
    where, cosines, sines = turns(where_ref, frequency_ref)
    rotary = turned(latents_ref[:, LATENT:].astype(jnp.float32), cosines, sines)
    lane = lax.broadcasted_iota(jnp.int32, rotary.shape, 1)
    high, low = position_parts(where)
    tail = jnp.where(lane == 0, high, jnp.where(lane == 1, low, 0.0))
    last = jnp.concatenate([rotary, tail], axis=1).astype(jnp.bfloat16)
    for copy in range(out_ref.shape[0]):
        out_ref[copy, :, :LATENT] = latents_ref[:, :LATENT]
        out_ref[copy, :, LATENT:] = last


def query_kernel(where_ref, frequency_ref, queries_ref, out_ref):
    where, cosines, sines = turns(where_ref, frequency_ref)
    lane = lax.broadcasted_iota(jnp.int32, sines.shape, 1)
    high, low = position_parts(where)
    tail = jnp.where(lane == 2, high, jnp.where(lane == 3, low, 0.0))
    for h in range(queries_ref.shape[0]):
        rotary = turned(queries_ref[h, :, LATENT:].astype(jnp.float32), cosines, sines)
        out_ref[h, :, :LATENT] = queries_ref[h, :, :LATENT]
        out_ref[h, :, LATENT:] = jnp.concatenate([rotary, tail], axis=1).astype(jnp.bfloat16)


def prepare(kernel, positions, rows, copies):
    half = np.exp(np.arange(ROPE // 2) * (-2.0 * math.log(10000.0) / ROPE))
    frequency = jnp.asarray(np.concatenate([half, half])[None], jnp.float32)
    return pl.pallas_call(
        kernel,
        out_shape=jax.ShapeDtypeStruct((copies, rows.shape[-2], WIDTH), jnp.bfloat16),
        compiler_params=pltpu.CompilerParams(vmem_limit_bytes=VMEM),
    )(positions.reshape(1, -1), frequency, rows)


def shift_z(x, by):
    perm = []
    for z in range(8):
        to = (z + by) % 8
        source = ((z % 4) // 2 * 2 + z % 2) * 2 + z // 4
        target = ((to % 4) // 2 * 2 + to % 2) * 2 + to // 4
        perm.append((source, target))
    return lax.ppermute(x, ("zh_lat", "zl_lat", "z_hi"), perm)


def swap(x, axis):
    return lax.ppermute(x, axis, [(0, 1), (1, 0)])


def attend_kernel(blocks, first, last, *refs):
    ends_ref, q_ref = refs[0], refs[1]
    key_refs = refs[2 : 2 + blocks]
    rest = refs[2 + blocks :]
    if not first:
        m_in, l_in, acc_in = rest[:3]
        rest = rest[3:]
    if last:
        up_ref, out_ref = rest
    else:
        m_out, l_out, acc_out = rest
    heads, toks, _ = q_ref.shape
    rows = heads * toks
    meta = q_ref[0, :, LATENT:].astype(jnp.float32)
    query_pos = meta[:, 66:67] * 64.0 + meta[:, 67:68]
    query_start = jnp.zeros_like(query_pos)
    for k in range(8):
        end = ends_ref[k].astype(jnp.float32)
        query_start = jnp.where(query_pos >= end, end, query_start)
    first_end = ends_ref[0].astype(jnp.float32)
    q = q_ref[...].reshape(rows, WIDTH)
    lane = lax.broadcasted_iota(jnp.int32, (toks, 128), 1)
    pick = jnp.where(lane == 64, 64.0, jnp.where(lane == 65, 1.0, 0.0)).astype(jnp.bfloat16)
    scores = []
    for key_ref in key_refs:
        keys = key_ref[...]
        key_pos = lax.dot_general(
            pick, keys[:, LATENT:], NT, preferred_element_type=jnp.float32
        )
        visible = (key_pos <= query_pos) & ((key_pos >= query_start) | (key_pos < first_end))
        raw = lax.dot_general(q, keys, NT, preferred_element_type=jnp.float32)
        raw = raw.reshape(heads, toks, keys.shape[0])
        scores.append(jnp.where(visible[None], raw, HIDDEN).reshape(rows, keys.shape[0]))
    top = functools.reduce(jnp.maximum, [jnp.max(s, axis=1, keepdims=True) for s in scores])
    if not first:
        old = m_in[...].reshape(rows, 128)[:, :1]
        top = jnp.maximum(top, old)
        fade = jnp.exp2((old - top) * LOG2_SCALE)
    total = 0.0
    mixed = 0.0
    for key_ref, s in zip(key_refs, scores):
        weights = jnp.exp2((s - top) * LOG2_SCALE)
        total = total + jnp.sum(weights, axis=1, keepdims=True)
        mixed = mixed + jnp.dot(
            weights.astype(jnp.bfloat16), key_ref[:, :LATENT], preferred_element_type=jnp.float32
        )
    if not first:
        total = total + fade * l_in[...].reshape(rows, 128)[:, :1]
        mixed = mixed + fade * acc_in[...].reshape(rows, LATENT)
    if not last:
        m_out[...] = jnp.broadcast_to(top, (rows, 128)).reshape(heads, toks, 128)
        l_out[...] = jnp.broadcast_to(total, (rows, 128)).reshape(heads, toks, 128)
        acc_out[...] = mixed.reshape(heads, toks, LATENT)
        return
    context = (mixed / total).astype(jnp.bfloat16).reshape(heads, toks, LATENT)
    level = (top * LOG2_SCALE + jnp.log2(total)).reshape(heads, toks, 1)
    half = toks // 2
    for h in range(heads):
        part = jnp.dot(context[h], up_ref[h], preferred_element_type=jnp.float32)
        at = slice(h * 128, h * 128 + 128)
        spread = jnp.broadcast_to(level[h], (toks, 128))
        for side in range(2):
            out_ref[side, 0, :, at] = part[side * half : (side + 1) * half]
            out_ref[side, 1, :, at] = spread[side * half : (side + 1) * half]


def attend(ends, q, keys, carry=None, up=None, group=2, weight=1):
    heads, toks, _ = q.shape
    first, last = carry is None, up is not None
    per_head = lambda width: pl.BlockSpec((group, toks, width), lambda i: (i, 0, 0))
    in_specs = [pl.BlockSpec(memory_space=pltpu.SMEM), per_head(WIDTH)]
    in_specs += [pl.BlockSpec(k.shape, lambda i: (0, 0)) for k in keys]
    args = [ends, q, *keys]
    state_specs = [per_head(128), per_head(128), per_head(LATENT)]
    if not first:
        in_specs += state_specs
        args += list(carry)
    if last:
        in_specs.append(pl.BlockSpec((group, LATENT, 128), lambda i: (i, 0, 0)))
        args.append(up)
        out_shape = jax.ShapeDtypeStruct((2, 2, toks // 2, heads * 128), jnp.float32)
        out_specs = pl.BlockSpec((2, 2, toks // 2, group * 128), lambda i: (0, 0, 0, i))
    else:
        out_shape = [
            jax.ShapeDtypeStruct((heads, toks, w), jnp.float32) for w in (128, 128, LATENT)
        ]
        out_specs = state_specs
    count = sum(k.shape[0] for k in keys)
    rows = heads * toks
    return pl.pallas_call(
        functools.partial(attend_kernel, len(keys), first, last),
        grid=(heads // group,),
        in_specs=in_specs,
        out_specs=out_specs,
        out_shape=out_shape,
        compiler_params=pltpu.CompilerParams(vmem_limit_bytes=VMEM),
        cost_estimate=pl.CostEstimate(
            flops=2 * weight * rows * count * (WIDTH + LATENT),
            bytes_accessed=weight * (2 * count * WIDTH + rows * 4096),
            transcendentals=weight * rows * count,
        ),
    )(*args)


def project_kernel(slots_ref, v_ref, w_ref, *refs):
    out_ref = refs[-1]
    core = slots_ref[1]
    part = lax.dot_general(v_ref[...], w_ref[0], NT, preferred_element_type=jnp.float32)
    toks = part.shape[0] // 2
    part = part.astype(jnp.bfloat16)
    out_ref[0, 0, core] = part[:toks]
    out_ref[0, 0, 1 - core] = part[toks:]


def project(near, core, v, w, into=None):
    blocks, cols, depth = w.shape
    toks = v.shape[0] // 2
    in_specs = [
        pl.BlockSpec(v.shape, lambda i, slots: (0, 0)),
        pl.BlockSpec((1, cols, depth), lambda i, slots: (i, 0, 0)),
    ]
    args = [jnp.stack([near, core]), v, w]
    if into is not None:
        in_specs.append(pl.BlockSpec(memory_space=pl.ANY))
        args.append(into)
    return pl.pallas_call(
        project_kernel,
        grid_spec=pltpu.PrefetchScalarGridSpec(
            num_scalar_prefetch=1,
            grid=(blocks,),
            in_specs=in_specs,
            out_specs=pl.BlockSpec(
                (1, 1, 2, toks, cols), lambda i, slots: (i, slots[0], 0, 0, 0)
            ),
        ),
        out_shape=jax.ShapeDtypeStruct((blocks, 2, 2, toks, cols), jnp.bfloat16),
        input_output_aliases={} if into is None else {3: 0},
        compiler_params=pltpu.CompilerParams(vmem_limit_bytes=VMEM),
        cost_estimate=pl.CostEstimate(
            flops=4 * toks * blocks * cols * depth,
            bytes_accessed=2 * blocks * cols * depth,
            transcendentals=0,
        ),
    )(*args)


def add_heads_kernel(parts_ref, out_ref):
    heads = parts_ref.shape[0]
    for near in range(2):
        total = []
        for core in range(2):
            t = parts_ref[0, near, core].astype(jnp.float32)
            for h in range(1, heads):
                t += parts_ref[h, near, core].astype(jnp.float32)
            total.append(t.astype(out_ref.dtype))
        for far in range(2):
            at = far * 256 + near * 128
            lanes = slice(far * 64, far * 64 + 64)
            out_ref[:, at : at + 128] = jnp.concatenate([t[:, lanes] for t in total], axis=1)


def add_heads(parts):
    toks, cols = parts.shape[3:]
    return pl.pallas_call(
        add_heads_kernel,
        out_shape=jax.ShapeDtypeStruct((toks, 4 * cols), parts.dtype),
        compiler_params=pltpu.CompilerParams(vmem_limit_bytes=VMEM),
    )(parts)


def pair_kernel(far_ref, own_ref, other_ref, _, out_ref):
    far = far_ref[0]
    out_ref[0, far] = own_ref[...]
    out_ref[0, 1 - far] = other_ref[...]


def pair(far, own, other, earlier, copies):
    corner = earlier.reshape(-1, earlier.shape[-1])
    whole = pl.BlockSpec(own.shape, lambda i: (0, 0))
    return pl.pallas_call(
        pair_kernel,
        grid=(copies,),
        in_specs=[
            pl.BlockSpec(memory_space=pltpu.SMEM),
            whole,
            whole,
            pl.BlockSpec((16, 128), lambda i: (0, 0)),
        ],
        out_specs=pl.BlockSpec((1, 2) + own.shape, lambda i: (i, 0, 0, 0)),
        out_shape=jax.ShapeDtypeStruct((copies, 2) + own.shape, own.dtype),
    )(far, own, other, corner)


def on_device(queries, latents, positions, lengths, value_up, out_weight):
    toks, heads, width = queries.shape
    ends = jnp.cumsum(lengths).astype(jnp.int32)
    core = lax.axis_index("core").astype(jnp.int32)
    far = lax.axis_index("zh_lat").astype(jnp.int32)
    near = lax.axis_index("zl_lat").astype(jnp.int32)

    key_rows = prepare(key_kernel, positions, latents, 8)
    along_y = lax.all_to_all(key_rows, "y", 0, 0).reshape(8 * toks, WIDTH)

    q_own = prepare(query_kernel, positions, queries.transpose(1, 0, 2), heads)
    q = jnp.concatenate([q_own, swap(q_own, "core")], axis=1)

    w = out_weight.T
    w = pair(far.reshape(1), w, swap(w, "zh_lat"), q, 8)
    w = lax.all_to_all(w, "y", 0, 0)
    w = w.reshape(8, -1, w.shape[3])

    from_left = shift_z(along_y, 1)
    from_right = shift_z(along_y, -1)
    carry = attend(ends, q, [along_y], group=8, weight=8)
    middle = along_y.shape[0] // 2
    across_left = shift_z(from_left[:middle], 1)
    across_right = shift_z(from_right[middle:], -1)
    carry = attend(ends, q, [from_left, from_right], carry, group=8, weight=8)

    both = attend(ends, q, [across_left, across_right], carry, value_up)
    theirs = swap(both, "core")
    values = []
    for side in range(2):
        (part_a, level_a), (part_b, level_b) = both[side], theirs[1 - side]
        level = jnp.maximum(level_a, level_b)
        share_a, share_b = jnp.exp2(level_a - level), jnp.exp2(level_b - level)
        values.append((part_a * share_a + part_b * share_b) / (share_a + share_b))
    values = jnp.concatenate(values, axis=0).astype(jnp.bfloat16)
    partial = project(near, core, values, w)
    partial = project(1 - near, core, swap(values, "zl_lat"), w, partial)
    arrived = lax.all_to_all(
        partial.reshape((32,) + partial.shape[3:]), ("z_hi", "x", "zl_lat", "core"), 0, 0
    )
    return add_heads(arrived.reshape(partial.shape))


def solution(mesh):
    grid = Mesh(
        mesh.devices.reshape(8, 2, 2, 2, 2, 4), ("y", "zh_lat", "zl_lat", "core", "z_hi", "x")
    )
    seq, head = ("y", "zh_lat", "zl_lat", "core"), ("z_hi", "x")
    placed = (
        P(seq, head, None),
        P(seq, None),
        P(seq),
        P(),
        P(head, None, None),
        P(head, seq),
    )
    return jax.shard_map(
        on_device, mesh=grid, in_specs=placed, out_specs=P(seq, head), check_vma=False
    )
```

```python
import functools
import math

import jax
import jax.numpy as jnp
from jax import lax
from jax.experimental import pallas as pl
from jax.experimental.pallas import tpu as pltpu
from jax.sharding import Mesh, PartitionSpec as P

LATENT = 512
ROPE = 64
WIDTH = 640
SCALE = 192.0 ** (-0.5)
LOG2_SCALE = SCALE * math.log2(math.e)
HIDDEN = -1e30
VMEM = 48 * 1024 * 1024
NT = (((1,), (1,)), ((), ()))
WHOLE = pl.BlockSpec(memory_space=pltpu.VMEM)


def turns(where_ref):
    toks = where_ref.shape[1]
    row = lax.broadcasted_iota(jnp.int32, (toks, toks), 0)
    column = lax.broadcasted_iota(jnp.int32, (toks, toks), 1)
    spread = jnp.broadcast_to(where_ref[...], (toks, toks))
    where = jnp.sum(jnp.where(row == column, spread, 0).astype(jnp.float32), axis=1, keepdims=True)
    lane = lax.broadcasted_iota(jnp.int32, (toks, ROPE), 1)
    pair = (lane % (ROPE // 2)).astype(jnp.float32)
    angles = where * jnp.exp(pair * (-2.0 * math.log(10000.0) / ROPE))
    sines = jnp.sin(angles)
    return where, jnp.cos(angles), jnp.where(lane < ROPE // 2, -sines, sines)


def turned(rotary, cosines, sines):
    half = ROPE // 2
    other = jnp.concatenate([rotary[:, half:], rotary[:, :half]], axis=1)
    return rotary * cosines + other * sines


def position_parts(where):
    high = jnp.floor(where * (1.0 / 64.0))
    return high, where - 64.0 * high


def key_kernel(where_ref, latents_ref, out_ref):
    where, cosines, sines = turns(where_ref)
    rotary = turned(latents_ref[:, LATENT:].astype(jnp.float32), cosines, sines)
    lane = lax.broadcasted_iota(jnp.int32, rotary.shape, 1)
    high, low = position_parts(where)
    tail = jnp.where(lane == 0, high, jnp.where(lane == 1, low, 0.0))
    last = jnp.concatenate([rotary, tail], axis=1).astype(jnp.bfloat16)
    for copy in range(out_ref.shape[0]):
        out_ref[copy, :, :LATENT] = latents_ref[:, :LATENT]
        out_ref[copy, :, LATENT:] = last


def query_kernel(where_ref, queries_ref, out_ref):
    where, cosines, sines = turns(where_ref)
    lane = lax.broadcasted_iota(jnp.int32, sines.shape, 1)
    high, low = position_parts(where)
    tail = jnp.where(lane == 2, high, jnp.where(lane == 3, low, 0.0))
    for h in range(queries_ref.shape[0]):
        rotary = turned(queries_ref[h, :, LATENT:].astype(jnp.float32), cosines, sines)
        out_ref[h, :, :LATENT] = queries_ref[h, :, :LATENT]
        out_ref[h, :, LATENT:] = jnp.concatenate([rotary, tail], axis=1).astype(jnp.bfloat16)


def prepare(kernel, positions, rows, copies):
    return pl.pallas_call(
        kernel,
        in_specs=[WHOLE] * 2,
        out_specs=WHOLE,
        out_shape=jax.ShapeDtypeStruct((copies, rows.shape[-2], WIDTH), jnp.bfloat16),
        compiler_params=pltpu.CompilerParams(vmem_limit_bytes=VMEM),
    )(positions.reshape(1, -1), rows)


def shift_z(x):
    perm = []
    for z in range(8):
        for core in range(2):
            to = (z + 1 - 2 * core) % 8
            source = ((z % 4) * 2 + core) * 2 + z // 4
            target = ((to % 4) * 2 + core) * 2 + to // 4
            perm.append((source, target))
    return lax.ppermute(x, ("zh_lat", "zl_lat", "core", "z_hi"), perm)


def swap(x, axis):
    return lax.ppermute(x, axis, [(0, 1), (1, 0)])


def attend_kernel(group, first, last, ends_ref, q_ref, key_ref, up_ref, *refs):
    if not first:
        top_in, total_in, part_in = refs[:3]
        refs = refs[3:]
    if last:
        (out_ref,) = refs
    else:
        top_out, total_out, part_out = refs
    heads, toks, _ = q_ref.shape
    half = toks // 2
    meta = q_ref[0, :, LATENT:].astype(jnp.float32)
    query_pos = meta[:, 66:67] * 64.0 + meta[:, 67:68]
    query_start = jnp.zeros_like(query_pos)
    for k in range(8):
        end = ends_ref[k].astype(jnp.float32)
        query_start = jnp.where(query_pos >= end, end, query_start)
    first_end = ends_ref[0].astype(jnp.float32)
    lane = lax.broadcasted_iota(jnp.int32, (toks, 128), 1)
    pick = jnp.where(lane == 64, 64.0, jnp.where(lane == 65, 1.0, 0.0)).astype(jnp.bfloat16)
    key_pos = lax.dot_general(
        pick, key_ref[:, LATENT:], NT, preferred_element_type=jnp.float32
    )
    visible = (key_pos <= query_pos) & ((key_pos >= query_start) | (key_pos < first_end))
    count = key_ref.shape[0]
    rows = group * toks
    levels = jnp.zeros((toks, 128), jnp.float32)
    for at in range(0, heads, group):
        some = slice(at, at + group)
        raw = lax.dot_general(
            q_ref[some].reshape(rows, WIDTH), key_ref[...], NT, preferred_element_type=jnp.float32
        )
        raw = raw.reshape(group, toks, count)
        scores = jnp.where(visible[None], raw, HIDDEN).reshape(rows, count)
        wide = lambda column: jnp.broadcast_to(column, (rows, 128))
        top = wide(jnp.max(scores, axis=1, keepdims=True))
        if not first:
            old = top_in[some].reshape(rows, 128)
            top = jnp.maximum(top, old)
            fade = jnp.exp2((old - top) * LOG2_SCALE)
        weights = jnp.exp2((scores - jnp.concatenate([top] * (count // 128), axis=1)) * LOG2_SCALE)
        total = wide(jnp.sum(weights, axis=1, keepdims=True))
        if not first:
            total = total + fade * total_in[some].reshape(rows, 128)
        context = jnp.dot(
            weights.astype(jnp.bfloat16), key_ref[:, :LATENT], preferred_element_type=jnp.float32
        ).astype(jnp.bfloat16)
        if last:
            inverse = 1.0 / total
            level = top * LOG2_SCALE + jnp.log2(total)
            high = level.astype(jnp.bfloat16).astype(jnp.float32)
            middle = (level - high).astype(jnp.bfloat16).astype(jnp.float32)
            low = level - high - middle
        else:
            top_out[some] = top.reshape(group, toks, 128)
            total_out[some] = total.reshape(group, toks, 128)
        for h in range(group):
            mine = slice(h * toks, h * toks + toks)
            part = jnp.dot(context[mine], up_ref[at + h], preferred_element_type=jnp.float32)
            if not first:
                part = part + fade[mine] * part_in[at + h]
            if not last:
                part_out[at + h] = part
                continue
            part = (part * inverse[mine]).astype(jnp.bfloat16)
            lanes = slice((at + h) * 128, (at + h) * 128 + 128)
            for side in range(2):
                out_ref[side, :, lanes] = part[side * half : (side + 1) * half]
            for piece, value in enumerate((high, middle, low)):
                levels = jnp.where(lane == 3 * (at + h) + piece, value[mine], levels)
    if last:
        levels = levels.astype(jnp.bfloat16)
        for side in range(2):
            out_ref[side, :, heads * 128 :] = levels[side * half : (side + 1) * half]


def attend(ends, q, keys, up, carry=None, last=False, group=8, weight=1):
    heads, toks, _ = q.shape
    first = carry is None
    args = [ends, q, keys, up] + list(carry or ())
    if last:
        out_shape = jax.ShapeDtypeStruct((2, toks // 2, heads * 128 + 128), jnp.bfloat16)
    else:
        out_shape = [jax.ShapeDtypeStruct((heads, toks, 128), jnp.float32)] * 3
    rows, count = heads * toks, keys.shape[0]
    return pl.pallas_call(
        functools.partial(attend_kernel, group, first, last),
        in_specs=[pl.BlockSpec(memory_space=pltpu.SMEM)] + [WHOLE] * (len(args) - 1),
        out_specs=WHOLE if last else [WHOLE] * 3,
        out_shape=out_shape,
        compiler_params=pltpu.CompilerParams(vmem_limit_bytes=VMEM),
        cost_estimate=pl.CostEstimate(
            flops=2 * weight * rows * count * (WIDTH + LATENT),
            bytes_accessed=weight * (2 * count * WIDTH + rows * 4096),
            transcendentals=weight * rows * count,
        ),
    )(*args)


def merge_kernel(own_ref, other_ref, out_ref):
    _, toks, width = own_ref.shape
    wide = width - 128
    lane = lax.broadcasted_iota(jnp.int32, (128, wide), 0)
    head = lax.broadcasted_iota(jnp.int32, (128, wide), 1) // 128
    spread = ((lane >= 3 * head) & (lane < 3 * head + 3)).astype(jnp.float32).astype(jnp.bfloat16)
    for side in range(2):
        refs = (own_ref, side), (other_ref, 1 - side)
        own, other = [
            jnp.dot(r[s, :, wide:], spread, preferred_element_type=jnp.float32) for r, s in refs
        ]
        top = jnp.maximum(own, other)
        own, other = jnp.exp2(own - top), jnp.exp2(other - top)
        own_part, other_part = [r[s, :, :wide].astype(jnp.float32) for r, s in refs]
        out_ref[side * toks : (side + 1) * toks, :] = (
            (own_part * own + other_part * other) * (1.0 / (own + other))
        ).astype(out_ref.dtype)


def merge(own, other):
    _, toks, width = own.shape
    return pl.pallas_call(
        merge_kernel,
        in_specs=[WHOLE] * 2,
        out_specs=WHOLE,
        out_shape=jax.ShapeDtypeStruct((2 * toks, width - 128), own.dtype),
        compiler_params=pltpu.CompilerParams(vmem_limit_bytes=VMEM),
    )(own, other)


def project_kernel(slots_ref, v_ref, w_ref, *refs):
    out_ref = refs[-1]
    near, core = slots_ref[0], slots_ref[1]
    toks = v_ref.shape[0] // 2
    for y in range(w_ref.shape[0]):
        part = lax.dot_general(v_ref[...], w_ref[y], NT, preferred_element_type=jnp.float32)
        part = part.astype(jnp.bfloat16)
        out_ref[y, near, core] = part[:toks]
        out_ref[y, near, 1 - core] = part[toks:]


def project(near, core, v, w, into=None):
    blocks, cols, depth = w.shape
    toks = v.shape[0] // 2
    args = [jnp.stack([near, core]), v, w] + ([] if into is None else [into])
    return pl.pallas_call(
        project_kernel,
        in_specs=[pl.BlockSpec(memory_space=pltpu.SMEM)] + [WHOLE] * (len(args) - 1),
        out_specs=WHOLE,
        out_shape=jax.ShapeDtypeStruct((blocks, 2, 2, toks, cols), jnp.bfloat16),
        input_output_aliases={} if into is None else {3: 0},
        compiler_params=pltpu.CompilerParams(vmem_limit_bytes=VMEM),
        cost_estimate=pl.CostEstimate(
            flops=4 * toks * blocks * cols * depth,
            bytes_accessed=2 * blocks * cols * depth,
            transcendentals=0,
        ),
    )(*args)


def add_heads_kernel(parts_ref, out_ref):
    heads = parts_ref.shape[0]
    for near in range(2):
        total = []
        for core in range(2):
            t = parts_ref[0, near, core].astype(jnp.float32)
            for h in range(1, heads):
                t += parts_ref[h, near, core].astype(jnp.float32)
            total.append(t.astype(out_ref.dtype))
        for far in range(2):
            at = far * 256 + near * 128
            lanes = slice(far * 64, far * 64 + 64)
            out_ref[:, at : at + 128] = jnp.concatenate([t[:, lanes] for t in total], axis=1)


def add_heads(parts):
    toks, cols = parts.shape[3:]
    return pl.pallas_call(
        add_heads_kernel,
        in_specs=[WHOLE],
        out_specs=WHOLE,
        out_shape=jax.ShapeDtypeStruct((toks, 4 * cols), parts.dtype),
        compiler_params=pltpu.CompilerParams(vmem_limit_bytes=VMEM),
    )(parts)


def pair_kernel(far_ref, own_ref, other_ref, _, out_ref):
    far = far_ref[0]
    out_ref[0, far] = own_ref[...]
    out_ref[0, 1 - far] = other_ref[...]


def pair(far, own, other, earlier, copies):
    corner = earlier.reshape(-1, earlier.shape[-1])
    whole = pl.BlockSpec(own.shape, lambda i: (0, 0))
    return pl.pallas_call(
        pair_kernel,
        grid=(copies,),
        in_specs=[
            pl.BlockSpec(memory_space=pltpu.SMEM),
            whole,
            whole,
            pl.BlockSpec((16, 128), lambda i: (0, 0)),
        ],
        out_specs=pl.BlockSpec((1, 2) + own.shape, lambda i: (i, 0, 0, 0)),
        out_shape=jax.ShapeDtypeStruct((copies, 2) + own.shape, own.dtype),
    )(far, own, other, corner)


def on_device(queries, latents, positions, lengths, value_up, out_weight):
    toks, heads, width = queries.shape
    ends = jnp.cumsum(lengths).astype(jnp.int32)
    core = lax.axis_index("core").astype(jnp.int32)
    far = lax.axis_index("zh_lat").astype(jnp.int32)
    near = lax.axis_index("zl_lat").astype(jnp.int32)

    key_rows = prepare(key_kernel, positions, latents, 8)
    along_y = lax.all_to_all(key_rows, "y", 0, 0).reshape(8 * toks, WIDTH)

    q_own = prepare(query_kernel, positions, queries.transpose(1, 0, 2), heads)
    q = jnp.concatenate([q_own, swap(q_own, "core")], axis=1)

    w = out_weight.T
    w = pair(far.reshape(1), w, swap(w, "zh_lat"), q, 8)
    w = lax.all_to_all(w, "y", 0, 0)
    w = w.reshape(8, -1, w.shape[3])

    next_own = shift_z(along_y)
    next_other = shift_z(swap(along_y, "core"))
    beyond = shift_z(next_own)
    carry = attend(ends, q, along_y, value_up, weight=8)
    carry = attend(ends, q, next_own, value_up, carry, weight=8)
    carry = attend(ends, q, next_other, value_up, carry, weight=8)
    part = attend(ends, q, beyond, value_up, carry, last=True)

    values = merge(part, swap(part, "core"))

    partial = project(near, core, values, w)
    partial = project(1 - near, core, swap(values, "zl_lat"), w, partial)
    arrived = lax.all_to_all(
        partial.reshape((32,) + partial.shape[3:]), ("z_hi", "x", "zl_lat", "core"), 0, 0
    )
    return add_heads(arrived.reshape(partial.shape))


def solution(mesh):
    grid = Mesh(
        mesh.devices.reshape(8, 2, 2, 2, 2, 4), ("y", "zh_lat", "zl_lat", "core", "z_hi", "x")
    )
    seq, head = ("y", "zh_lat", "zl_lat", "core"), ("z_hi", "x")
    placed = (
        P(seq, head, None),
        P(seq, None),
        P(seq),
        P(),
        P(head, None, None),
        P(head, seq),
    )
    return jax.shard_map(
        on_device, mesh=grid, in_specs=placed, out_specs=P(seq, head), check_vma=False
    )
```

```python
import functools
import math

import jax
import jax.numpy as jnp
from jax import lax
from jax.experimental import pallas as pl
from jax.experimental.pallas import tpu as pltpu
from jax.sharding import Mesh, PartitionSpec as P

LATENT = 512
ROPE = 64
WIDTH = 640
SCALE = 192.0 ** (-0.5)
LOG2_SCALE = SCALE * math.log2(math.e)
HIDDEN = -1e30
VMEM = 48 * 1024 * 1024
NT = (((1,), (1,)), ((), ()))
WHOLE = pl.BlockSpec(memory_space=pltpu.VMEM)
ANYWHERE = pl.BlockSpec(memory_space=pl.ANY)


def turns(where_ref):
    toks = where_ref.shape[1]
    row = lax.broadcasted_iota(jnp.int32, (toks, toks), 0)
    column = lax.broadcasted_iota(jnp.int32, (toks, toks), 1)
    spread = jnp.broadcast_to(where_ref[...], (toks, toks))
    where = jnp.sum(jnp.where(row == column, spread, 0).astype(jnp.float32), axis=1, keepdims=True)
    lane = lax.broadcasted_iota(jnp.int32, (toks, ROPE), 1)
    pair = (lane % (ROPE // 2)).astype(jnp.float32)
    angles = where * jnp.exp(pair * (-2.0 * math.log(10000.0) / ROPE))
    sines = jnp.sin(angles)
    return where, jnp.cos(angles), jnp.where(lane < ROPE // 2, -sines, sines)


def turned(rotary, cosines, sines):
    half = ROPE // 2
    other = jnp.concatenate([rotary[:, half:], rotary[:, :half]], axis=1)
    return rotary * cosines + other * sines


def position_parts(where):
    high = jnp.floor(where * (1.0 / 64.0))
    return high, where - 64.0 * high


def key_kernel(where_hbm, latents_hbm, out_hbm, where_ref, latents_ref, rows_ref, in_sems, out_sems):
    arrivals = [
        pltpu.make_async_copy(where_hbm, where_ref, in_sems.at[0]),
        pltpu.make_async_copy(latents_hbm, latents_ref, in_sems.at[1]),
    ]
    for arrival in arrivals:
        arrival.start()
    for arrival in arrivals:
        arrival.wait()
    where, cosines, sines = turns(where_ref)
    rotary = turned(latents_ref[:, LATENT:].astype(jnp.float32), cosines, sines)
    lane = lax.broadcasted_iota(jnp.int32, rotary.shape, 1)
    high, low = position_parts(where)
    tail = jnp.where(lane == 0, high, jnp.where(lane == 1, low, 0.0))
    rows_ref[:, :LATENT] = latents_ref[:, :LATENT]
    rows_ref[:, LATENT:] = jnp.concatenate([rotary, tail], axis=1).astype(jnp.bfloat16)
    send_copies(rows_ref, out_hbm, out_sems)


def send_copies(ref, out_hbm, sems):
    copies = [pltpu.make_async_copy(ref, out_hbm.at[i], sems.at[i]) for i in range(out_hbm.shape[0])]
    for copy in copies:
        copy.start()
    for copy in copies:
        copy.wait()


def prepare_keys(positions, latents, copies):
    toks, width = latents.shape
    return pl.pallas_call(
        key_kernel,
        in_specs=[pl.BlockSpec(memory_space=pltpu.HBM)] * 2,
        out_specs=ANYWHERE,
        out_shape=jax.ShapeDtypeStruct((copies, toks, WIDTH), latents.dtype),
        scratch_shapes=[
            pltpu.VMEM((1, toks), jnp.int32),
            pltpu.VMEM((toks, width), latents.dtype),
            pltpu.VMEM((toks, WIDTH), latents.dtype),
            pltpu.SemaphoreType.DMA((2,)),
            pltpu.SemaphoreType.DMA((copies,)),
        ],
        compiler_params=pltpu.CompilerParams(vmem_limit_bytes=VMEM),
    )(positions.reshape(1, -1), latents)


def query_kernel(where_ref, queries_ref, out_ref):
    where, cosines, sines = turns(where_ref)
    lane = lax.broadcasted_iota(jnp.int32, sines.shape, 1)
    high, low = position_parts(where)
    tail = jnp.where(lane == 2, high, jnp.where(lane == 3, low, 0.0))
    for h in range(queries_ref.shape[0]):
        rotary = turned(queries_ref[h, :, LATENT:].astype(jnp.float32), cosines, sines)
        out_ref[h, :, :LATENT] = queries_ref[h, :, :LATENT]
        out_ref[h, :, LATENT:] = jnp.concatenate([rotary, tail], axis=1).astype(jnp.bfloat16)


def prepare_queries(positions, queries):
    heads, toks, _ = queries.shape
    return pl.pallas_call(
        query_kernel,
        in_specs=[WHOLE] * 2,
        out_specs=WHOLE,
        out_shape=jax.ShapeDtypeStruct((heads, toks, WIDTH), queries.dtype),
        compiler_params=pltpu.CompilerParams(vmem_limit_bytes=VMEM),
    )(positions.reshape(1, -1), queries)


def shift_z(x):
    perm = []
    for z in range(8):
        for core in range(2):
            to = (z + 1 - 2 * core) % 8
            source = ((z % 4) * 2 + core) * 2 + z // 4
            target = ((to % 4) * 2 + core) * 2 + to // 4
            perm.append((source, target))
    return lax.ppermute(x, ("zh_lat", "zl_lat", "core", "z_hi"), perm)


def swap(x, axis):
    return lax.ppermute(x, axis, [(0, 1), (1, 0)])


def attend_kernel(group, first, last, ends_ref, q_ref, key_ref, up_ref, *refs):
    if not first:
        top_in, total_in, part_in = refs[:3]
        refs = refs[3:]
    if last:
        (out_ref,) = refs
    else:
        top_out, total_out, part_out = refs
    heads, toks, _ = q_ref.shape
    half = toks // 2
    meta = q_ref[0, :, LATENT:].astype(jnp.float32)
    query_pos = meta[:, 66:67] * 64.0 + meta[:, 67:68]
    query_start = jnp.zeros_like(query_pos)
    for k in range(8):
        end = ends_ref[k].astype(jnp.float32)
        query_start = jnp.where(query_pos >= end, end, query_start)
    first_end = ends_ref[0].astype(jnp.float32)
    lane = lax.broadcasted_iota(jnp.int32, (toks, 128), 1)
    pick = jnp.where(lane == 64, 64.0, jnp.where(lane == 65, 1.0, 0.0)).astype(jnp.bfloat16)
    key_pos = lax.dot_general(
        pick, key_ref[:, LATENT:], NT, preferred_element_type=jnp.float32
    )
    visible = (key_pos <= query_pos) & ((key_pos >= query_start) | (key_pos < first_end))
    count = key_ref.shape[0]
    rows = group * toks
    levels = jnp.zeros((toks, 128), jnp.float32)
    for at in range(0, heads, group):
        some = slice(at, at + group)
        raw = lax.dot_general(
            q_ref[some].reshape(rows, WIDTH), key_ref[...], NT, preferred_element_type=jnp.float32
        )
        raw = raw.reshape(group, toks, count)
        scores = jnp.where(visible[None], raw, HIDDEN).reshape(rows, count)
        wide = lambda column: jnp.broadcast_to(column, (rows, 128))
        top = wide(jnp.max(scores, axis=1, keepdims=True))
        if not first:
            old = top_in[some].reshape(rows, 128)
            top = jnp.maximum(top, old)
            fade = jnp.exp2((old - top) * LOG2_SCALE)
        weights = jnp.exp2((scores - jnp.concatenate([top] * (count // 128), axis=1)) * LOG2_SCALE)
        total = wide(jnp.sum(weights, axis=1, keepdims=True))
        if not first:
            total = total + fade * total_in[some].reshape(rows, 128)
        context = jnp.dot(
            weights.astype(jnp.bfloat16), key_ref[:, :LATENT], preferred_element_type=jnp.float32
        ).astype(jnp.bfloat16)
        if last:
            inverse = 1.0 / total
            level = top * LOG2_SCALE + jnp.log2(total)
            high = level.astype(jnp.bfloat16).astype(jnp.float32)
            middle = (level - high).astype(jnp.bfloat16).astype(jnp.float32)
            low = level - high - middle
        else:
            top_out[some] = top.reshape(group, toks, 128)
            total_out[some] = total.reshape(group, toks, 128)
        for h in range(group):
            mine = slice(h * toks, h * toks + toks)
            part = jnp.dot(context[mine], up_ref[at + h], preferred_element_type=jnp.float32)
            if not first:
                part = part + fade[mine] * part_in[at + h]
            if not last:
                part_out[at + h] = part
                continue
            part = (part * inverse[mine]).astype(jnp.bfloat16)
            lanes = slice((at + h) * 128, (at + h) * 128 + 128)
            for side in range(2):
                out_ref[side, :, lanes] = part[side * half : (side + 1) * half]
            for piece, value in enumerate((high, middle, low)):
                levels = jnp.where(lane == 3 * (at + h) + piece, value[mine], levels)
    if last:
        levels = levels.astype(jnp.bfloat16)
        for side in range(2):
            out_ref[side, :, heads * 128 :] = levels[side * half : (side + 1) * half]


def attend(ends, q, keys, up, carry=None, last=False, group=8, weight=1):
    heads, toks, _ = q.shape
    first = carry is None
    args = [ends, q, keys, up] + list(carry or ())
    if last:
        out_shape = jax.ShapeDtypeStruct((2, toks // 2, heads * 128 + 128), jnp.bfloat16)
    else:
        out_shape = [jax.ShapeDtypeStruct((heads, toks, 128), jnp.float32)] * 3
    rows, count = heads * toks, keys.shape[0]
    return pl.pallas_call(
        functools.partial(attend_kernel, group, first, last),
        in_specs=[pl.BlockSpec(memory_space=pltpu.SMEM)] + [WHOLE] * (len(args) - 1),
        out_specs=WHOLE if last else [WHOLE] * 3,
        out_shape=out_shape,
        compiler_params=pltpu.CompilerParams(vmem_limit_bytes=VMEM),
        cost_estimate=pl.CostEstimate(
            flops=2 * weight * rows * count * (WIDTH + LATENT),
            bytes_accessed=weight * (2 * count * WIDTH + rows * 4096),
            transcendentals=weight * rows * count,
        ),
    )(*args)


def merge_kernel(own_ref, other_ref, out_ref):
    _, toks, width = own_ref.shape
    wide = width - 128
    lane = lax.broadcasted_iota(jnp.int32, (128, wide), 0)
    head = lax.broadcasted_iota(jnp.int32, (128, wide), 1) // 128
    spread = ((lane >= 3 * head) & (lane < 3 * head + 3)).astype(jnp.float32).astype(jnp.bfloat16)
    for side in range(2):
        refs = (own_ref, side), (other_ref, 1 - side)
        own, other = [
            jnp.dot(r[s, :, wide:], spread, preferred_element_type=jnp.float32) for r, s in refs
        ]
        top = jnp.maximum(own, other)
        own, other = jnp.exp2(own - top), jnp.exp2(other - top)
        own_part, other_part = [r[s, :, :wide].astype(jnp.float32) for r, s in refs]
        out_ref[side * toks : (side + 1) * toks, :] = (
            (own_part * own + other_part * other) * (1.0 / (own + other))
        ).astype(out_ref.dtype)


def merge(own, other):
    _, toks, width = own.shape
    return pl.pallas_call(
        merge_kernel,
        in_specs=[WHOLE] * 2,
        out_specs=WHOLE,
        out_shape=jax.ShapeDtypeStruct((2 * toks, width - 128), own.dtype),
        compiler_params=pltpu.CompilerParams(vmem_limit_bytes=VMEM),
    )(own, other)


def project_kernel(slots_ref, v_ref, w_ref, out_ref):
    near, core = slots_ref[0], slots_ref[1]
    toks = v_ref.shape[0] // 4
    for y in range(w_ref.shape[0]):
        part = lax.dot_general(v_ref[...], w_ref[y], NT, preferred_element_type=jnp.float32)
        part = part.astype(jnp.bfloat16)
        for k in range(4):
            at_near = near if k < 2 else 1 - near
            at_core = core if k % 2 == 0 else 1 - core
            out_ref[at_near, y, at_core] = part[k * toks : (k + 1) * toks]


def project(near, core, v, w):
    blocks, cols, depth = w.shape
    toks = v.shape[0] // 4
    return pl.pallas_call(
        project_kernel,
        in_specs=[pl.BlockSpec(memory_space=pltpu.SMEM)] + [WHOLE] * 2,
        out_specs=WHOLE,
        out_shape=jax.ShapeDtypeStruct((2, blocks, 2, toks, cols), jnp.bfloat16),
        compiler_params=pltpu.CompilerParams(vmem_limit_bytes=VMEM),
        cost_estimate=pl.CostEstimate(
            flops=8 * toks * blocks * cols * depth,
            bytes_accessed=2 * blocks * cols * depth,
            transcendentals=0,
        ),
    )(jnp.stack([near, core]), v, w)


def add_heads_kernel(core_ref, parts_ref, keep_ref, give_ref):
    core = core_ref[0]
    for near in range(2):
        for whose, out_ref in ((core, keep_ref), (1 - core, give_ref)):
            total = parts_ref[near, 0, whose].astype(jnp.float32)
            for h in range(1, parts_ref.shape[1]):
                total += parts_ref[near, h, whose].astype(jnp.float32)
            out_ref[near] = total.astype(out_ref.dtype)


def add_heads(core, parts):
    half = jax.ShapeDtypeStruct((2,) + parts.shape[3:], parts.dtype)
    return pl.pallas_call(
        add_heads_kernel,
        in_specs=[pl.BlockSpec(memory_space=pltpu.SMEM), WHOLE],
        out_specs=[WHOLE] * 2,
        out_shape=[half] * 2,
        compiler_params=pltpu.CompilerParams(vmem_limit_bytes=VMEM),
    )(core, parts)


def lay_out_kernel(core_ref, own_ref, other_ref, out_ref):
    first = core_ref[0] == 0
    for near in range(2):
        own, other = own_ref[near], other_ref[near]
        for far in range(2):
            lanes = slice(far * 64, far * 64 + 64)
            at = far * 256 + near * 128
            out_ref[:, at : at + 128] = jnp.where(
                first,
                jnp.concatenate([own[:, lanes], other[:, lanes]], axis=1),
                jnp.concatenate([other[:, lanes], own[:, lanes]], axis=1),
            )


def lay_out(core, own, other):
    _, toks, cols = own.shape
    return pl.pallas_call(
        lay_out_kernel,
        in_specs=[pl.BlockSpec(memory_space=pltpu.SMEM)] + [WHOLE] * 2,
        out_specs=WHOLE,
        out_shape=jax.ShapeDtypeStruct((toks, 4 * cols), own.dtype),
        compiler_params=pltpu.CompilerParams(vmem_limit_bytes=VMEM),
    )(core, own, other)


def pair_kernel(far_ref, own_ref, other_ref, _, out_hbm, both_ref, sems):
    far = far_ref[0]
    both_ref[far] = own_ref[...]
    both_ref[1 - far] = other_ref[...]
    send_copies(both_ref, out_hbm, sems)


def pair(far, own, other, earlier, copies):
    corner = earlier.reshape(-1, earlier.shape[-1])[:16, :128]
    return pl.pallas_call(
        pair_kernel,
        in_specs=[pl.BlockSpec(memory_space=pltpu.SMEM)] + [WHOLE] * 3,
        out_specs=ANYWHERE,
        out_shape=jax.ShapeDtypeStruct((copies, 2) + own.shape, own.dtype),
        scratch_shapes=[
            pltpu.VMEM((2,) + own.shape, own.dtype),
            pltpu.SemaphoreType.DMA((copies,)),
        ],
        compiler_params=pltpu.CompilerParams(vmem_limit_bytes=VMEM),
    )(far, own, other, corner)


def on_device(queries, latents, positions, lengths, value_up, out_weight):
    toks, heads, width = queries.shape
    ends = jnp.cumsum(lengths).astype(jnp.int32)
    core = lax.axis_index("core").astype(jnp.int32)
    far = lax.axis_index("zh_lat").astype(jnp.int32)
    near = lax.axis_index("zl_lat").astype(jnp.int32)

    key_rows = prepare_keys(positions, latents, 8)
    along_y = lax.all_to_all(key_rows, "y", 0, 0).reshape(8 * toks, WIDTH)

    q_own = prepare_queries(positions, queries.transpose(1, 0, 2))
    q = jnp.concatenate([q_own, swap(q_own, "core")], axis=1)

    w = out_weight.T
    w = pair(far.reshape(1), w, swap(w, "zh_lat"), q, 8)
    w = lax.all_to_all(w, "y", 0, 0)
    w = w.reshape(8, -1, w.shape[3])

    next_own = shift_z(along_y)
    next_other = shift_z(swap(along_y, "core"))
    beyond = shift_z(next_own)
    carry = attend(ends, q, along_y, value_up, weight=3)
    carry = attend(ends, q, next_own, value_up, carry, weight=3)
    carry = attend(ends, q, next_other, value_up, carry, weight=3)
    part = attend(ends, q, beyond, value_up, carry, last=True)

    values = merge(part, swap(part, "core"))

    v = jnp.concatenate([values, swap(values, "zl_lat")], axis=0)

    partial = project(near, core, v, w)
    arrived = lax.all_to_all(
        partial.reshape((16,) + partial.shape[2:]), ("zl_lat", "z_hi", "x"), 0, 0
    )
    keep, give = add_heads(core.reshape(1), arrived.reshape(partial.shape))
    return lay_out(core.reshape(1), keep, swap(give, "core"))


def solution(mesh):
    grid = Mesh(
        mesh.devices.reshape(8, 2, 2, 2, 2, 4), ("y", "zh_lat", "zl_lat", "core", "z_hi", "x")
    )
    seq, head = ("y", "zh_lat", "zl_lat", "core"), ("z_hi", "x")
    placed = (
        P(seq, head, None),
        P(seq, None),
        P(seq),
        P(),
        P(head, None, None),
        P(head, seq),
    )
    return jax.shard_map(
        on_device, mesh=grid, in_specs=placed, out_specs=P(seq, head), check_vma=False
    )
```

```python
import functools
import math

import jax
import jax.numpy as jnp
from jax import lax
from jax.experimental import pallas as pl
from jax.experimental.pallas import tpu as pltpu
from jax.sharding import Mesh, PartitionSpec as P

LATENT = 512
ROPE = 64
WIDTH = 640
SCALE = 192.0 ** (-0.5)
LOG2_SCALE = SCALE * math.log2(math.e)
HIDDEN = -1e30
VMEM = 48 * 1024 * 1024
NT = (((1,), (1,)), ((), ()))
WHOLE = pl.BlockSpec(memory_space=pltpu.VMEM)
ANYWHERE = pl.BlockSpec(memory_space=pl.ANY)


def turns(where_ref):
    toks = where_ref.shape[1]
    row = lax.broadcasted_iota(jnp.int32, (toks, toks), 0)
    column = lax.broadcasted_iota(jnp.int32, (toks, toks), 1)
    spread = jnp.broadcast_to(where_ref[...], (toks, toks))
    where = jnp.sum(jnp.where(row == column, spread, 0).astype(jnp.float32), axis=1, keepdims=True)
    lane = lax.broadcasted_iota(jnp.int32, (toks, ROPE), 1)
    pair = (lane % (ROPE // 2)).astype(jnp.float32)
    angles = where * jnp.exp(pair * (-2.0 * math.log(10000.0) / ROPE))
    sines = jnp.sin(angles)
    return where, jnp.cos(angles), jnp.where(lane < ROPE // 2, -sines, sines)


def turned(rotary, cosines, sines):
    half = ROPE // 2
    other = jnp.concatenate([rotary[:, half:], rotary[:, :half]], axis=1)
    return rotary * cosines + other * sines


def position_parts(where):
    high = jnp.floor(where * (1.0 / 64.0))
    return high, where - 64.0 * high


def key_kernel(where_hbm, latents_hbm, out_hbm, where_ref, latents_ref, rows_ref, in_sems, out_sems):
    arrivals = [
        pltpu.make_async_copy(where_hbm, where_ref, in_sems.at[0]),
        pltpu.make_async_copy(latents_hbm, latents_ref, in_sems.at[1]),
    ]
    for arrival in arrivals:
        arrival.start()
    for arrival in arrivals:
        arrival.wait()
    where, cosines, sines = turns(where_ref)
    rotary = turned(latents_ref[:, LATENT:].astype(jnp.float32), cosines, sines)
    lane = lax.broadcasted_iota(jnp.int32, rotary.shape, 1)
    high, low = position_parts(where)
    tail = jnp.where(lane == 0, high, jnp.where(lane == 1, low, 0.0))
    rows_ref[:, :LATENT] = latents_ref[:, :LATENT]
    rows_ref[:, LATENT:] = jnp.concatenate([rotary, tail], axis=1).astype(jnp.bfloat16)
    send_copies(rows_ref, out_hbm, out_sems)


def send_copies(ref, out_hbm, sems):
    copies = [pltpu.make_async_copy(ref, out_hbm.at[i], sems.at[i]) for i in range(out_hbm.shape[0])]
    for copy in copies:
        copy.start()
    for copy in copies:
        copy.wait()


def prepare_keys(positions, latents, copies):
    toks, width = latents.shape
    return pl.pallas_call(
        key_kernel,
        in_specs=[pl.BlockSpec(memory_space=pltpu.HBM)] * 2,
        out_specs=ANYWHERE,
        out_shape=jax.ShapeDtypeStruct((copies, toks, WIDTH), latents.dtype),
        scratch_shapes=[
            pltpu.VMEM((1, toks), jnp.int32),
            pltpu.VMEM((toks, width), latents.dtype),
            pltpu.VMEM((toks, WIDTH), latents.dtype),
            pltpu.SemaphoreType.DMA((2,)),
            pltpu.SemaphoreType.DMA((copies,)),
        ],
        compiler_params=pltpu.CompilerParams(vmem_limit_bytes=60 * 1024 * 1024),
    )(positions.reshape(1, -1), latents)


def query_kernel(where_ref, queries_ref, out_ref):
    where, cosines, sines = turns(where_ref)
    lane = lax.broadcasted_iota(jnp.int32, sines.shape, 1)
    high, low = position_parts(where)
    tail = jnp.where(lane == 2, high, jnp.where(lane == 3, low, 0.0))
    for h in range(queries_ref.shape[0]):
        rotary = turned(queries_ref[h, :, LATENT:].astype(jnp.float32), cosines, sines)
        out_ref[h, :, :LATENT] = queries_ref[h, :, :LATENT]
        out_ref[h, :, LATENT:] = jnp.concatenate([rotary, tail], axis=1).astype(jnp.bfloat16)


def prepare_queries(positions, queries):
    heads, toks, _ = queries.shape
    return pl.pallas_call(
        query_kernel,
        in_specs=[WHOLE] * 2,
        out_specs=WHOLE,
        out_shape=jax.ShapeDtypeStruct((heads, toks, WIDTH), queries.dtype),
        compiler_params=pltpu.CompilerParams(vmem_limit_bytes=VMEM),
    )(positions.reshape(1, -1), queries)


def shift_z(x):
    perm = []
    for z in range(8):
        for core in range(2):
            to = (z + 1 - 2 * core) % 8
            source = ((z % 4) * 2 + core) * 2 + z // 4
            target = ((to % 4) * 2 + core) * 2 + to // 4
            perm.append((source, target))
    return lax.ppermute(x, ("zh_lat", "zl_lat", "core", "z_hi"), perm)


def swap(x, axis):
    return lax.ppermute(x, axis, [(0, 1), (1, 0)])


def attend_kernel(group, first, last, ends_ref, q_ref, key_ref, up_ref, *refs):
    if not first:
        top_in, total_in, part_in = refs[:3]
        refs = refs[3:]
    if last:
        (out_ref,) = refs
    else:
        top_out, total_out, part_out = refs
    heads, toks, _ = q_ref.shape
    half = toks // 2
    meta = q_ref[0, :, LATENT:].astype(jnp.float32)
    query_pos = meta[:, 66:67] * 64.0 + meta[:, 67:68]
    query_start = jnp.zeros_like(query_pos)
    for k in range(8):
        end = ends_ref[k].astype(jnp.float32)
        query_start = jnp.where(query_pos >= end, end, query_start)
    first_end = ends_ref[0].astype(jnp.float32)
    lane = lax.broadcasted_iota(jnp.int32, (toks, 128), 1)
    pick = jnp.where(lane == 64, 64.0, jnp.where(lane == 65, 1.0, 0.0)).astype(jnp.bfloat16)
    key_pos = lax.dot_general(
        pick, key_ref[:, LATENT:], NT, preferred_element_type=jnp.float32
    )
    visible = (key_pos <= query_pos) & ((key_pos >= query_start) | (key_pos < first_end))
    count = key_ref.shape[0]
    rows = group * toks
    levels = jnp.zeros((toks, 128), jnp.float32)
    for at in range(0, heads, group):
        some = slice(at, at + group)
        raw = lax.dot_general(
            q_ref[some].reshape(rows, WIDTH), key_ref[...], NT, preferred_element_type=jnp.float32
        )
        raw = raw.reshape(group, toks, count)
        scores = jnp.where(visible[None], raw, HIDDEN).reshape(rows, count)
        wide = lambda column: jnp.broadcast_to(column, (rows, 128))
        top = wide(jnp.max(scores, axis=1, keepdims=True))
        if not first:
            old = top_in[some].reshape(rows, 128)
            top = jnp.maximum(top, old)
            fade = jnp.exp2((old - top) * LOG2_SCALE)
        weights = jnp.exp2((scores - jnp.concatenate([top] * (count // 128), axis=1)) * LOG2_SCALE)
        total = wide(jnp.sum(weights, axis=1, keepdims=True))
        if not first:
            total = total + fade * total_in[some].reshape(rows, 128)
        context = jnp.dot(
            weights.astype(jnp.bfloat16), key_ref[:, :LATENT], preferred_element_type=jnp.float32
        ).astype(jnp.bfloat16)
        if last:
            inverse = 1.0 / total
            level = top * LOG2_SCALE + jnp.log2(total)
            high = level.astype(jnp.bfloat16).astype(jnp.float32)
            middle = (level - high).astype(jnp.bfloat16).astype(jnp.float32)
            low = level - high - middle
        else:
            top_out[some] = top.reshape(group, toks, 128)
            total_out[some] = total.reshape(group, toks, 128)
        for h in range(group):
            mine = slice(h * toks, h * toks + toks)
            part = jnp.dot(context[mine], up_ref[at + h], preferred_element_type=jnp.float32)
            if not first:
                part = part + fade[mine] * part_in[at + h]
            if not last:
                part_out[at + h] = part
                continue
            part = (part * inverse[mine]).astype(jnp.bfloat16)
            lanes = slice((at + h) * 128, (at + h) * 128 + 128)
            for side in range(2):
                out_ref[side, :, lanes] = part[side * half : (side + 1) * half]
            for piece, value in enumerate((high, middle, low)):
                levels = jnp.where(lane == 3 * (at + h) + piece, value[mine], levels)
    if last:
        levels = levels.astype(jnp.bfloat16)
        for side in range(2):
            out_ref[side, :, heads * 128 :] = levels[side * half : (side + 1) * half]


def attend(ends, q, keys, up, carry=None, last=False, group=8, weight=1):
    heads, toks, _ = q.shape
    first = carry is None
    args = [ends, q, keys, up] + list(carry or ())
    if last:
        out_shape = jax.ShapeDtypeStruct((2, toks // 2, heads * 128 + 128), jnp.bfloat16)
    else:
        out_shape = [jax.ShapeDtypeStruct((heads, toks, 128), jnp.float32)] * 3
    rows, count = heads * toks, keys.shape[0]
    return pl.pallas_call(
        functools.partial(attend_kernel, group, first, last),
        in_specs=[pl.BlockSpec(memory_space=pltpu.SMEM)] + [WHOLE] * (len(args) - 1),
        out_specs=WHOLE if last else [WHOLE] * 3,
        out_shape=out_shape,
        compiler_params=pltpu.CompilerParams(vmem_limit_bytes=VMEM),
        cost_estimate=pl.CostEstimate(
            flops=2 * weight * rows * count * (WIDTH + LATENT),
            bytes_accessed=weight * (2 * count * WIDTH + rows * 4096),
            transcendentals=weight * rows * count,
        ),
    )(*args)


def merge_kernel(own_ref, other_ref, out_ref):
    _, toks, width = own_ref.shape
    wide = width - 128
    lane = lax.broadcasted_iota(jnp.int32, (128, wide), 0)
    head = lax.broadcasted_iota(jnp.int32, (128, wide), 1) // 128
    spread = ((lane >= 3 * head) & (lane < 3 * head + 3)).astype(jnp.float32).astype(jnp.bfloat16)
    for side in range(2):
        refs = (own_ref, side), (other_ref, 1 - side)
        own, other = [
            jnp.dot(r[s, :, wide:], spread, preferred_element_type=jnp.float32) for r, s in refs
        ]
        top = jnp.maximum(own, other)
        own, other = jnp.exp2(own - top), jnp.exp2(other - top)
        own_part, other_part = [r[s, :, :wide].astype(jnp.float32) for r, s in refs]
        out_ref[side * toks : (side + 1) * toks, :] = (
            (own_part * own + other_part * other) * (1.0 / (own + other))
        ).astype(out_ref.dtype)


def merge(own, other):
    _, toks, width = own.shape
    return pl.pallas_call(
        merge_kernel,
        in_specs=[WHOLE] * 2,
        out_specs=WHOLE,
        out_shape=jax.ShapeDtypeStruct((2 * toks, width - 128), own.dtype),
        compiler_params=pltpu.CompilerParams(vmem_limit_bytes=VMEM),
    )(own, other)


def project_kernel(slots_ref, v_ref, w_ref, out_ref):
    near, core = slots_ref[0], slots_ref[1]
    toks = v_ref.shape[0] // 4
    for y in range(w_ref.shape[0]):
        part = lax.dot_general(v_ref[...], w_ref[y], NT, preferred_element_type=jnp.float32)
        part = part.astype(jnp.bfloat16)
        for k in range(4):
            at_near = near if k < 2 else 1 - near
            at_core = core if k % 2 == 0 else 1 - core
            out_ref[y % 4, at_near, at_core, y // 4] = part[k * toks : (k + 1) * toks]


def project(near, core, v, w):
    blocks, cols, depth = w.shape
    toks = v.shape[0] // 4
    return pl.pallas_call(
        project_kernel,
        in_specs=[pl.BlockSpec(memory_space=pltpu.SMEM)] + [WHOLE] * 2,
        out_specs=WHOLE,
        out_shape=jax.ShapeDtypeStruct((4, 2, 2, blocks // 4, toks, cols), jnp.bfloat16),
        compiler_params=pltpu.CompilerParams(vmem_limit_bytes=VMEM),
        cost_estimate=pl.CostEstimate(
            flops=8 * toks * blocks * cols * depth,
            bytes_accessed=2 * blocks * cols * depth,
            transcendentals=0,
        ),
    )(jnp.stack([near, core]), v, w)


def add_x_kernel(here_ref, parts_ref, keep_ref, give_ref):
    here = here_ref[0]
    for whose, out_ref in ((1 - here, give_ref), (here, keep_ref)):
        for near in range(2):
            total = []
            for core in range(2):
                t = parts_ref[0, near, core, whose].astype(jnp.float32)
                for x in range(1, parts_ref.shape[0]):
                    t += parts_ref[x, near, core, whose].astype(jnp.float32)
                total.append(t)
            for far in range(2):
                at = far * 256 + near * 128
                lanes = slice(far * 64, far * 64 + 64)
                out_ref[:, at : at + 128] = jnp.concatenate(
                    [t[:, lanes] for t in total], axis=1
                ).astype(out_ref.dtype)


def add_x(here, parts):
    toks, cols = parts.shape[4:]
    return pl.pallas_call(
        add_x_kernel,
        in_specs=[pl.BlockSpec(memory_space=pltpu.SMEM), WHOLE],
        out_specs=[WHOLE] * 2,
        out_shape=[
            jax.ShapeDtypeStruct((toks, 4 * cols), jnp.float32),
            jax.ShapeDtypeStruct((toks, 4 * cols), parts.dtype),
        ],
        compiler_params=pltpu.CompilerParams(vmem_limit_bytes=VMEM),
    )(here, parts)


def pair_kernel(far_ref, own_ref, other_ref, _, out_hbm, both_ref, sems):
    far = far_ref[0]
    both_ref[far] = own_ref[...]
    both_ref[1 - far] = other_ref[...]
    send_copies(both_ref, out_hbm, sems)


def pair(far, own, other, earlier, copies):
    corner = earlier.reshape(-1, earlier.shape[-1])[:16, :128]
    return pl.pallas_call(
        pair_kernel,
        in_specs=[pl.BlockSpec(memory_space=pltpu.SMEM)] + [WHOLE] * 3,
        out_specs=ANYWHERE,
        out_shape=jax.ShapeDtypeStruct((copies, 2) + own.shape, own.dtype),
        scratch_shapes=[
            pltpu.VMEM((2,) + own.shape, own.dtype),
            pltpu.SemaphoreType.DMA((copies,)),
        ],
        compiler_params=pltpu.CompilerParams(vmem_limit_bytes=VMEM),
    )(far, own, other, corner)


def on_device(queries, latents, positions, lengths, value_up, out_weight):
    toks, heads, width = queries.shape
    ends = jnp.cumsum(lengths).astype(jnp.int32)
    core = lax.axis_index("core").astype(jnp.int32)
    far = lax.axis_index("zh_lat").astype(jnp.int32)
    near = lax.axis_index("zl_lat").astype(jnp.int32)

    key_rows = prepare_keys(positions, latents, 8)
    along_y = lax.all_to_all(key_rows, "y", 0, 0).reshape(8 * toks, WIDTH)

    q_own = prepare_queries(positions, queries.transpose(1, 0, 2))
    q = jnp.concatenate([q_own, swap(q_own, "core")], axis=1)

    w = out_weight.T
    w = pair(far.reshape(1), w, swap(w, "zh_lat"), q, 8)
    w = lax.all_to_all(w, "y", 0, 0)
    w = w.reshape(8, -1, w.shape[3])

    next_own = shift_z(along_y)
    next_other = shift_z(swap(along_y, "core"))
    beyond = shift_z(next_own)
    carry = attend(ends, q, along_y, value_up, weight=3)
    carry = attend(ends, q, next_own, value_up, carry, weight=3)
    carry = attend(ends, q, next_other, value_up, carry, weight=3)
    part = attend(ends, q, beyond, value_up, carry, last=True)

    values = merge(part, swap(part, "core"))

    v = jnp.concatenate([values, swap(values, "zl_lat")], axis=0)

    partial = project(near, core, v, w)
    parts = lax.all_to_all(
        partial.reshape((16,) + partial.shape[3:]), ("x", "zl_lat", "core"), 0, 0
    )
    z_hi = lax.axis_index("z_hi").astype(jnp.int32)
    keep, give = add_x(z_hi.reshape(1), parts.reshape(partial.shape))
    return (keep + swap(give, "z_hi").astype(jnp.float32)).astype(jnp.bfloat16)


def solution(mesh):
    grid = Mesh(
        mesh.devices.reshape(8, 2, 2, 2, 2, 4), ("y", "zh_lat", "zl_lat", "core", "z_hi", "x")
    )
    seq, head = ("y", "zh_lat", "zl_lat", "core"), ("z_hi", "x")
    placed = (
        P(seq, head, None),
        P(seq, None),
        P(seq),
        P(),
        P(head, None, None),
        P(head, seq),
    )
    return jax.shard_map(
        on_device, mesh=grid, in_specs=placed, out_specs=P(seq, head), check_vma=False
    )
```

```python
import functools
import math

import jax
import jax.numpy as jnp
from jax import lax
from jax.experimental import pallas as pl
from jax.experimental.pallas import tpu as pltpu
from jax.sharding import Mesh, PartitionSpec as P

LATENT = 512
ROPE = 64
WIDTH = 640
SCALE = 192.0 ** (-0.5)
LOG2_SCALE = SCALE * math.log2(math.e)
HIDDEN = -1e30
VMEM = 48 * 1024 * 1024
NT = (((1,), (1,)), ((), ()))
WHOLE = pl.BlockSpec(memory_space=pltpu.VMEM)
ANYWHERE = pl.BlockSpec(memory_space=pl.ANY)


def turns(where_ref):
    toks = where_ref.shape[1]
    row = lax.broadcasted_iota(jnp.int32, (toks, toks), 0)
    column = lax.broadcasted_iota(jnp.int32, (toks, toks), 1)
    spread = jnp.broadcast_to(where_ref[...], (toks, toks))
    where = jnp.sum(jnp.where(row == column, spread, 0).astype(jnp.float32), axis=1, keepdims=True)
    lane = lax.broadcasted_iota(jnp.int32, (toks, ROPE), 1)
    pair = (lane % (ROPE // 2)).astype(jnp.float32)
    angles = where * jnp.exp(pair * (-2.0 * math.log(10000.0) / ROPE))
    sines = jnp.sin(angles)
    return where, jnp.cos(angles), jnp.where(lane < ROPE // 2, -sines, sines)


def turned(rotary, cosines, sines):
    half = ROPE // 2
    other = jnp.concatenate([rotary[:, half:], rotary[:, :half]], axis=1)
    return rotary * cosines + other * sines


def position_parts(where):
    high = jnp.floor(where * (1.0 / 64.0))
    return high, where - 64.0 * high


def key_kernel(where_hbm, latents_hbm, out_hbm, where_ref, latents_ref, rows_ref, in_sems, out_sems):
    arrivals = [
        pltpu.make_async_copy(where_hbm, where_ref, in_sems.at[0]),
        pltpu.make_async_copy(latents_hbm, latents_ref, in_sems.at[1]),
    ]
    for arrival in arrivals:
        arrival.start()
    for arrival in arrivals:
        arrival.wait()
    where, cosines, sines = turns(where_ref)
    rotary = turned(latents_ref[:, LATENT:].astype(jnp.float32), cosines, sines)
    lane = lax.broadcasted_iota(jnp.int32, rotary.shape, 1)
    high, low = position_parts(where)
    tail = jnp.where(lane == 0, high, jnp.where(lane == 1, low, 0.0))
    rows_ref[:, :LATENT] = latents_ref[:, :LATENT]
    rows_ref[:, LATENT:] = jnp.concatenate([rotary, tail], axis=1).astype(jnp.bfloat16)
    send_copies(rows_ref, out_hbm, out_sems)


def send_copies(ref, out_hbm, sems):
    copies = [pltpu.make_async_copy(ref, out_hbm.at[i], sems.at[i]) for i in range(out_hbm.shape[0])]
    for copy in copies:
        copy.start()
    for copy in copies:
        copy.wait()


def prepare_keys(positions, latents, copies):
    toks, width = latents.shape
    return pl.pallas_call(
        key_kernel,
        in_specs=[pl.BlockSpec(memory_space=pltpu.HBM)] * 2,
        out_specs=ANYWHERE,
        out_shape=jax.ShapeDtypeStruct((copies, toks, WIDTH), latents.dtype),
        scratch_shapes=[
            pltpu.VMEM((1, toks), jnp.int32),
            pltpu.VMEM((toks, width), latents.dtype),
            pltpu.VMEM((toks, WIDTH), latents.dtype),
            pltpu.SemaphoreType.DMA((2,)),
            pltpu.SemaphoreType.DMA((copies,)),
        ],
        compiler_params=pltpu.CompilerParams(vmem_limit_bytes=60 * 1024 * 1024),
    )(positions.reshape(1, -1), latents)


def query_kernel(where_ref, queries_ref, out_ref):
    where, cosines, sines = turns(where_ref)
    lane = lax.broadcasted_iota(jnp.int32, sines.shape, 1)
    high, low = position_parts(where)
    tail = jnp.where(lane == 2, high, jnp.where(lane == 3, low, 0.0))
    for h in range(queries_ref.shape[0]):
        rotary = turned(queries_ref[h, :, LATENT:].astype(jnp.float32), cosines, sines)
        out_ref[h, :, :LATENT] = queries_ref[h, :, :LATENT]
        out_ref[h, :, LATENT:] = jnp.concatenate([rotary, tail], axis=1).astype(jnp.bfloat16)


def prepare_queries(positions, queries):
    heads, toks, _ = queries.shape
    return pl.pallas_call(
        query_kernel,
        in_specs=[WHOLE] * 2,
        out_specs=WHOLE,
        out_shape=jax.ShapeDtypeStruct((heads, toks, WIDTH), queries.dtype),
        compiler_params=pltpu.CompilerParams(vmem_limit_bytes=VMEM),
    )(positions.reshape(1, -1), queries)


def shift_z(x):
    perm = []
    for z in range(8):
        for core in range(2):
            to = (z + 1 - 2 * core) % 8
            source = ((z % 4) * 2 + core) * 2 + z // 4
            target = ((to % 4) * 2 + core) * 2 + to // 4
            perm.append((source, target))
    return lax.ppermute(x, ("zh_lat", "zl_lat", "core", "z_hi"), perm)


def swap(x, axis):
    return lax.ppermute(x, axis, [(0, 1), (1, 0)])


def attend_kernel(group, first, last, ends_ref, q_ref, key_ref, up_ref, *refs):
    if first:
        key_hbm = key_ref
        top_out, total_out, part_out, key_ref, sem = refs
        arrival = pltpu.make_async_copy(key_hbm, key_ref, sem.at[0])
        arrival.start()
        arrival.wait()
    else:
        top_in, total_in, part_in = refs[:3]
        refs = refs[3:]
        if last:
            (out_ref,) = refs
        else:
            top_out, total_out, part_out = refs
    heads, toks, _ = q_ref.shape
    half = toks // 2
    meta = q_ref[0, :, LATENT:].astype(jnp.float32)
    query_pos = meta[:, 66:67] * 64.0 + meta[:, 67:68]
    query_start = jnp.zeros_like(query_pos)
    for k in range(8):
        end = ends_ref[k].astype(jnp.float32)
        query_start = jnp.where(query_pos >= end, end, query_start)
    first_end = ends_ref[0].astype(jnp.float32)
    lane = lax.broadcasted_iota(jnp.int32, (toks, 128), 1)
    pick = jnp.where(lane == 64, 64.0, jnp.where(lane == 65, 1.0, 0.0)).astype(jnp.bfloat16)
    key_pos = lax.dot_general(
        pick, key_ref[:, LATENT:], NT, preferred_element_type=jnp.float32
    )
    visible = (key_pos <= query_pos) & ((key_pos >= query_start) | (key_pos < first_end))
    count = key_ref.shape[0]
    rows = group * toks
    levels = jnp.zeros((toks, 128), jnp.float32)
    for at in range(0, heads, group):
        some = slice(at, at + group)
        raw = lax.dot_general(
            q_ref[some].reshape(rows, WIDTH), key_ref[...], NT, preferred_element_type=jnp.float32
        )
        raw = raw.reshape(group, toks, count)
        scores = jnp.where(visible[None], raw, HIDDEN).reshape(rows, count)
        wide = lambda column: jnp.broadcast_to(column, (rows, 128))
        top = wide(jnp.max(scores, axis=1, keepdims=True))
        if not first:
            old = top_in[some].reshape(rows, 128)
            top = jnp.maximum(top, old)
            fade = jnp.exp2((old - top) * LOG2_SCALE)
        weights = jnp.exp2((scores - jnp.concatenate([top] * (count // 128), axis=1)) * LOG2_SCALE)
        total = wide(jnp.sum(weights, axis=1, keepdims=True))
        if not first:
            total = total + fade * total_in[some].reshape(rows, 128)
        context = jnp.dot(
            weights.astype(jnp.bfloat16), key_ref[:, :LATENT], preferred_element_type=jnp.float32
        ).astype(jnp.bfloat16)
        if last:
            inverse = 1.0 / total
            level = top * LOG2_SCALE + jnp.log2(total)
            high = level.astype(jnp.bfloat16).astype(jnp.float32)
            middle = (level - high).astype(jnp.bfloat16).astype(jnp.float32)
            low = level - high - middle
        else:
            top_out[some] = top.reshape(group, toks, 128)
            total_out[some] = total.reshape(group, toks, 128)
        for h in range(group):
            mine = slice(h * toks, h * toks + toks)
            part = jnp.dot(context[mine], up_ref[at + h], preferred_element_type=jnp.float32)
            if not first:
                part = part + fade[mine] * part_in[at + h]
            if not last:
                part_out[at + h] = part
                continue
            part = (part * inverse[mine]).astype(jnp.bfloat16)
            lanes = slice((at + h) * 128, (at + h) * 128 + 128)
            for side in range(2):
                out_ref[side, :, lanes] = part[side * half : (side + 1) * half]
            for piece, value in enumerate((high, middle, low)):
                levels = jnp.where(lane == 3 * (at + h) + piece, value[mine], levels)
    if last:
        levels = levels.astype(jnp.bfloat16)
        for side in range(2):
            out_ref[side, :, heads * 128 :] = levels[side * half : (side + 1) * half]


def attend(ends, q, keys, up, carry=None, last=False, group=8, weight=1):
    heads, toks, _ = q.shape
    first = carry is None
    args = [ends, q, keys, up] + list(carry or ())
    if last:
        out_shape = jax.ShapeDtypeStruct((2, toks // 2, heads * 128 + 128), jnp.bfloat16)
    else:
        out_shape = [jax.ShapeDtypeStruct((heads, toks, 128), jnp.float32)] * 3
    rows, count = heads * toks, keys.shape[0]
    return pl.pallas_call(
        functools.partial(attend_kernel, group, first, last),
        in_specs=[
            pl.BlockSpec(memory_space=pltpu.SMEM),
            WHOLE,
            pl.BlockSpec(memory_space=pltpu.HBM) if first else WHOLE,
        ]
        + [WHOLE] * (len(args) - 3),
        out_specs=WHOLE if last else [WHOLE] * 3,
        out_shape=out_shape,
        scratch_shapes=[pltpu.VMEM(keys.shape, keys.dtype), pltpu.SemaphoreType.DMA((1,))]
        if first
        else [],
        compiler_params=pltpu.CompilerParams(
            vmem_limit_bytes=56 * 1024 * 1024 if first else VMEM
        ),
        cost_estimate=pl.CostEstimate(
            flops=2 * weight * rows * count * (WIDTH + LATENT),
            bytes_accessed=weight * (2 * count * WIDTH + rows * 4096),
            transcendentals=weight * rows * count,
        ),
    )(*args)


def merge_kernel(own_ref, other_ref, out_ref):
    _, toks, width = own_ref.shape
    wide = width - 128
    lane = lax.broadcasted_iota(jnp.int32, (128, wide), 0)
    head = lax.broadcasted_iota(jnp.int32, (128, wide), 1) // 128
    spread = ((lane >= 3 * head) & (lane < 3 * head + 3)).astype(jnp.float32).astype(jnp.bfloat16)
    for side in range(2):
        refs = (own_ref, side), (other_ref, 1 - side)
        own, other = [
            jnp.dot(r[s, :, wide:], spread, preferred_element_type=jnp.float32) for r, s in refs
        ]
        top = jnp.maximum(own, other)
        own, other = jnp.exp2(own - top), jnp.exp2(other - top)
        own_part, other_part = [r[s, :, :wide].astype(jnp.float32) for r, s in refs]
        out_ref[side * toks : (side + 1) * toks, :] = (
            (own_part * own + other_part * other) * (1.0 / (own + other))
        ).astype(out_ref.dtype)


def merge(own, other):
    _, toks, width = own.shape
    return pl.pallas_call(
        merge_kernel,
        in_specs=[WHOLE] * 2,
        out_specs=WHOLE,
        out_shape=jax.ShapeDtypeStruct((2 * toks, width - 128), own.dtype),
        compiler_params=pltpu.CompilerParams(vmem_limit_bytes=VMEM),
    )(own, other)


def project_kernel(slots_ref, v_ref, w_ref, out_ref):
    near, core = slots_ref[0], slots_ref[1]
    toks = v_ref.shape[0] // 4
    for y in range(w_ref.shape[0]):
        part = lax.dot_general(v_ref[...], w_ref[y], NT, preferred_element_type=jnp.float32)
        part = part.astype(jnp.bfloat16)
        for k in range(4):
            at_near = near if k < 2 else 1 - near
            at_core = core if k % 2 == 0 else 1 - core
            out_ref[y % 4, at_near, at_core, y // 4] = part[k * toks : (k + 1) * toks]


def project(near, core, v, w):
    blocks, cols, depth = w.shape
    toks = v.shape[0] // 4
    return pl.pallas_call(
        project_kernel,
        in_specs=[pl.BlockSpec(memory_space=pltpu.SMEM)] + [WHOLE] * 2,
        out_specs=WHOLE,
        out_shape=jax.ShapeDtypeStruct((4, 2, 2, blocks // 4, toks, cols), jnp.bfloat16),
        compiler_params=pltpu.CompilerParams(vmem_limit_bytes=VMEM),
        cost_estimate=pl.CostEstimate(
            flops=8 * toks * blocks * cols * depth,
            bytes_accessed=2 * blocks * cols * depth,
            transcendentals=0,
        ),
    )(jnp.stack([near, core]), v, w)


def add_x_kernel(here_ref, parts_ref, keep_ref, give_ref):
    here = here_ref[0]
    for whose, out_ref in ((1 - here, give_ref), (here, keep_ref)):
        for near in range(2):
            total = []
            for core in range(2):
                t = parts_ref[0, near, core, whose].astype(jnp.float32)
                for x in range(1, parts_ref.shape[0]):
                    t += parts_ref[x, near, core, whose].astype(jnp.float32)
                total.append(t)
            for far in range(2):
                at = far * 256 + near * 128
                lanes = slice(far * 64, far * 64 + 64)
                out_ref[:, at : at + 128] = jnp.concatenate(
                    [t[:, lanes] for t in total], axis=1
                ).astype(out_ref.dtype)


def add_x(here, parts):
    toks, cols = parts.shape[4:]
    return pl.pallas_call(
        add_x_kernel,
        in_specs=[pl.BlockSpec(memory_space=pltpu.SMEM), WHOLE],
        out_specs=[WHOLE] * 2,
        out_shape=[
            jax.ShapeDtypeStruct((toks, 4 * cols), jnp.float32),
            jax.ShapeDtypeStruct((toks, 4 * cols), parts.dtype),
        ],
        compiler_params=pltpu.CompilerParams(vmem_limit_bytes=VMEM),
    )(here, parts)


def pair_kernel(far_ref, own_ref, other_ref, _, out_hbm, both_ref, sems):
    far = far_ref[0]
    both_ref[far] = own_ref[...]
    both_ref[1 - far] = other_ref[...]
    send_copies(both_ref, out_hbm, sems)


def pair(far, own, other, earlier, copies):
    corner = earlier.reshape(-1, earlier.shape[-1])[:16, :128]
    return pl.pallas_call(
        pair_kernel,
        in_specs=[pl.BlockSpec(memory_space=pltpu.SMEM)] + [WHOLE] * 3,
        out_specs=ANYWHERE,
        out_shape=jax.ShapeDtypeStruct((copies, 2) + own.shape, own.dtype),
        scratch_shapes=[
            pltpu.VMEM((2,) + own.shape, own.dtype),
            pltpu.SemaphoreType.DMA((copies,)),
        ],
        compiler_params=pltpu.CompilerParams(vmem_limit_bytes=VMEM),
    )(far, own, other, corner)


def on_device(queries, latents, positions, lengths, value_up, out_weight):
    toks, heads, width = queries.shape
    ends = jnp.cumsum(lengths).astype(jnp.int32)
    core = lax.axis_index("core").astype(jnp.int32)
    far = lax.axis_index("zh_lat").astype(jnp.int32)
    near = lax.axis_index("zl_lat").astype(jnp.int32)

    key_rows = prepare_keys(positions, latents, 8)
    along_y = lax.all_to_all(key_rows, "y", 0, 0).reshape(8 * toks, WIDTH)

    q_own = prepare_queries(positions, queries.transpose(1, 0, 2))
    q = jnp.concatenate([q_own, swap(q_own, "core")], axis=1)

    w = out_weight.T
    w = pair(far.reshape(1), w, swap(w, "zh_lat"), q, 8)
    w = lax.all_to_all(w, "y", 0, 0)
    w = w.reshape(8, -1, w.shape[3])

    next_own = shift_z(along_y)
    next_other = shift_z(swap(along_y, "core"))
    beyond = shift_z(next_own)
    carry = attend(ends, q, along_y, value_up, weight=3)
    carry = attend(ends, q, next_own, value_up, carry, weight=3)
    carry = attend(ends, q, next_other, value_up, carry, weight=3)
    part = attend(ends, q, beyond, value_up, carry, last=True)

    values = merge(part, swap(part, "core"))

    v = jnp.concatenate([values, swap(values, "zl_lat")], axis=0)

    partial = project(near, core, v, w)
    parts = lax.all_to_all(
        partial.reshape((16,) + partial.shape[3:]), ("x", "zl_lat", "core"), 0, 0
    )
    z_hi = lax.axis_index("z_hi").astype(jnp.int32)
    keep, give = add_x(z_hi.reshape(1), parts.reshape(partial.shape))
    return (keep + swap(give, "z_hi").astype(jnp.float32)).astype(jnp.bfloat16)


def solution(mesh):
    grid = Mesh(
        mesh.devices.reshape(8, 2, 2, 2, 2, 4), ("y", "zh_lat", "zl_lat", "core", "z_hi", "x")
    )
    seq, head = ("y", "zh_lat", "zl_lat", "core"), ("z_hi", "x")
    placed = (
        P(seq, head, None),
        P(seq, None),
        P(seq),
        P(),
        P(head, None, None),
        P(head, seq),
    )
    return jax.shard_map(
        on_device, mesh=grid, in_specs=placed, out_specs=P(seq, head), check_vma=False
    )
```

```python
import functools
import math

import jax
import jax.numpy as jnp
from jax import lax
from jax.experimental import pallas as pl
from jax.experimental.pallas import tpu as pltpu
from jax.sharding import Mesh, PartitionSpec as P

LATENT = 512
ROPE = 64
WIDTH = 640
SCALE = 192.0 ** (-0.5)
LOG2_SCALE = SCALE * math.log2(math.e)
HIDDEN = -1e30
VMEM = 48 * 1024 * 1024
NT = (((1,), (1,)), ((), ()))
WHOLE = pl.BlockSpec(memory_space=pltpu.VMEM)
ANYWHERE = pl.BlockSpec(memory_space=pl.ANY)


def turns(where_ref):
    toks = where_ref.shape[1]
    row = lax.broadcasted_iota(jnp.int32, (toks, toks), 0)
    column = lax.broadcasted_iota(jnp.int32, (toks, toks), 1)
    spread = jnp.broadcast_to(where_ref[...], (toks, toks))
    where = jnp.sum(jnp.where(row == column, spread, 0).astype(jnp.float32), axis=1, keepdims=True)
    lane = lax.broadcasted_iota(jnp.int32, (toks, ROPE), 1)
    pair = (lane % (ROPE // 2)).astype(jnp.float32)
    angles = where * jnp.exp(pair * (-2.0 * math.log(10000.0) / ROPE))
    sines = jnp.sin(angles)
    return where, jnp.cos(angles), jnp.where(lane < ROPE // 2, -sines, sines)


def turned(rotary, cosines, sines):
    half = ROPE // 2
    other = jnp.concatenate([rotary[:, half:], rotary[:, :half]], axis=1)
    return rotary * cosines + other * sines


def position_parts(where):
    high = jnp.floor(where * (1.0 / 64.0))
    return high, where - 64.0 * high


def key_kernel(where_hbm, latents_hbm, out_hbm, where_ref, latents_ref, rows_ref, in_sems, out_sems):
    arrivals = [
        pltpu.make_async_copy(where_hbm, where_ref, in_sems.at[0]),
        pltpu.make_async_copy(latents_hbm, latents_ref, in_sems.at[1]),
    ]
    for arrival in arrivals:
        arrival.start()
    for arrival in arrivals:
        arrival.wait()
    where, cosines, sines = turns(where_ref)
    rotary = turned(latents_ref[:, LATENT:].astype(jnp.float32), cosines, sines)
    lane = lax.broadcasted_iota(jnp.int32, rotary.shape, 1)
    high, low = position_parts(where)
    tail = jnp.where(lane == 0, high, jnp.where(lane == 1, low, 0.0))
    rows_ref[:, :LATENT] = latents_ref[:, :LATENT]
    rows_ref[:, LATENT:] = jnp.concatenate([rotary, tail], axis=1).astype(jnp.bfloat16)
    send_copies(rows_ref, out_hbm, out_sems)


def send_copies(ref, out_hbm, sems):
    copies = [pltpu.make_async_copy(ref, out_hbm.at[i], sems.at[i]) for i in range(out_hbm.shape[0])]
    for copy in copies:
        copy.start()
    for copy in copies:
        copy.wait()


def prepare_keys(positions, latents, copies):
    toks, width = latents.shape
    return pl.pallas_call(
        key_kernel,
        in_specs=[pl.BlockSpec(memory_space=pltpu.HBM)] * 2,
        out_specs=ANYWHERE,
        out_shape=jax.ShapeDtypeStruct((copies, toks, WIDTH), latents.dtype),
        scratch_shapes=[
            pltpu.VMEM((1, toks), jnp.int32),
            pltpu.VMEM((toks, width), latents.dtype),
            pltpu.VMEM((toks, WIDTH), latents.dtype),
            pltpu.SemaphoreType.DMA((2,)),
            pltpu.SemaphoreType.DMA((copies,)),
        ],
        compiler_params=pltpu.CompilerParams(vmem_limit_bytes=60 * 1024 * 1024),
    )(positions.reshape(1, -1), latents)


def query_kernel(where_ref, queries_ref, out_ref):
    where, cosines, sines = turns(where_ref)
    lane = lax.broadcasted_iota(jnp.int32, sines.shape, 1)
    high, low = position_parts(where)
    tail = jnp.where(lane == 2, high, jnp.where(lane == 3, low, 0.0))
    for h in range(queries_ref.shape[0]):
        rotary = turned(queries_ref[h, :, LATENT:].astype(jnp.float32), cosines, sines)
        out_ref[h, :, :LATENT] = queries_ref[h, :, :LATENT]
        out_ref[h, :, LATENT:] = jnp.concatenate([rotary, tail], axis=1).astype(jnp.bfloat16)


def prepare_queries(positions, queries):
    heads, toks, _ = queries.shape
    return pl.pallas_call(
        query_kernel,
        in_specs=[WHOLE] * 2,
        out_specs=WHOLE,
        out_shape=jax.ShapeDtypeStruct((heads, toks, WIDTH), queries.dtype),
        compiler_params=pltpu.CompilerParams(vmem_limit_bytes=VMEM),
    )(positions.reshape(1, -1), queries)


def shift_z(x):
    perm = []
    for z in range(8):
        for core in range(2):
            to = (z + 1 - 2 * core) % 8
            source = ((z % 4) * 2 + core) * 2 + z // 4
            target = ((to % 4) * 2 + core) * 2 + to // 4
            perm.append((source, target))
    return lax.ppermute(x, ("zh_lat", "zl_lat", "core", "z_hi"), perm)


def swap(x, axis):
    return lax.ppermute(x, axis, [(0, 1), (1, 0)])


def attend_kernel(group, first, last, ends_ref, q_ref, key_ref, up_ref, *refs):
    if first:
        key_hbm = key_ref
        top_out, total_out, part_out, key_ref, sem = refs
        arrival = pltpu.make_async_copy(key_hbm, key_ref, sem.at[0])
        arrival.start()
        arrival.wait()
    else:
        top_in, total_in, part_in = refs[:3]
        refs = refs[3:]
        if last:
            (out_ref,) = refs
        else:
            top_out, total_out, part_out = refs
    heads, toks, _ = q_ref.shape
    half = toks // 2
    meta = q_ref[0, :, LATENT:].astype(jnp.float32)
    query_pos = meta[:, 66:67] * 64.0 + meta[:, 67:68]
    query_start = jnp.zeros_like(query_pos)
    for k in range(8):
        end = ends_ref[k].astype(jnp.float32)
        query_start = jnp.where(query_pos >= end, end, query_start)
    first_end = ends_ref[0].astype(jnp.float32)
    lane = lax.broadcasted_iota(jnp.int32, (toks, 128), 1)
    pick = jnp.where(lane == 64, 64.0, jnp.where(lane == 65, 1.0, 0.0)).astype(jnp.bfloat16)
    key_pos = lax.dot_general(
        pick, key_ref[:, LATENT:], NT, preferred_element_type=jnp.float32
    )
    visible = (key_pos <= query_pos) & ((key_pos >= query_start) | (key_pos < first_end))
    count = key_ref.shape[0]
    rows = group * toks
    levels = jnp.zeros((toks, 128), jnp.float32)
    for at in range(0, heads, group):
        some = slice(at, at + group)
        raw = lax.dot_general(
            q_ref[some].reshape(rows, WIDTH), key_ref[...], NT, preferred_element_type=jnp.float32
        )
        raw = raw.reshape(group, toks, count)
        scores = jnp.where(visible[None], raw, HIDDEN).reshape(rows, count)
        wide = lambda column: jnp.broadcast_to(column, (rows, 128))
        top = wide(jnp.max(scores, axis=1, keepdims=True))
        if not first:
            old = top_in[some].reshape(rows, 128)
            top = jnp.maximum(top, old)
            fade = jnp.exp2((old - top) * LOG2_SCALE)
        weights = jnp.exp2((scores - jnp.concatenate([top] * (count // 128), axis=1)) * LOG2_SCALE)
        total = wide(jnp.sum(weights, axis=1, keepdims=True))
        if not first:
            total = total + fade * total_in[some].reshape(rows, 128)
        context = jnp.dot(
            weights.astype(jnp.bfloat16), key_ref[:, :LATENT], preferred_element_type=jnp.float32
        ).astype(jnp.bfloat16)
        if last:
            inverse = 1.0 / total
            level = top * LOG2_SCALE + jnp.log2(total)
            high = level.astype(jnp.bfloat16).astype(jnp.float32)
            middle = (level - high).astype(jnp.bfloat16).astype(jnp.float32)
            low = level - high - middle
        else:
            top_out[some] = top.reshape(group, toks, 128)
            total_out[some] = total.reshape(group, toks, 128)
        for h in range(group):
            mine = slice(h * toks, h * toks + toks)
            part = jnp.dot(context[mine], up_ref[at + h], preferred_element_type=jnp.float32)
            if not first:
                part = part + fade[mine] * part_in[at + h]
            if not last:
                part_out[at + h] = part
                continue
            part = (part * inverse[mine]).astype(jnp.bfloat16)
            lanes = slice((at + h) * 128, (at + h) * 128 + 128)
            for side in range(2):
                out_ref[side, :, lanes] = part[side * half : (side + 1) * half]
            for piece, value in enumerate((high, middle, low)):
                levels = jnp.where(lane == 3 * (at + h) + piece, value[mine], levels)
    if last:
        levels = levels.astype(jnp.bfloat16)
        for side in range(2):
            out_ref[side, :, heads * 128 :] = levels[side * half : (side + 1) * half]


def attend(ends, q, keys, up, carry=None, last=False, group=8, weight=1):
    heads, toks, _ = q.shape
    first = carry is None
    args = [ends, q, keys, up] + list(carry or ())
    if last:
        out_shape = jax.ShapeDtypeStruct((2, toks // 2, heads * 128 + 128), jnp.bfloat16)
    else:
        out_shape = [jax.ShapeDtypeStruct((heads, toks, 128), jnp.float32)] * 3
    rows, count = heads * toks, keys.shape[0]
    return pl.pallas_call(
        functools.partial(attend_kernel, group, first, last),
        in_specs=[
            pl.BlockSpec(memory_space=pltpu.SMEM),
            WHOLE,
            pl.BlockSpec(memory_space=pltpu.HBM) if first else WHOLE,
        ]
        + [WHOLE] * (len(args) - 3),
        out_specs=WHOLE if last else [WHOLE] * 3,
        out_shape=out_shape,
        scratch_shapes=[pltpu.VMEM(keys.shape, keys.dtype), pltpu.SemaphoreType.DMA((1,))]
        if first
        else [],
        compiler_params=pltpu.CompilerParams(
            vmem_limit_bytes=56 * 1024 * 1024 if first else VMEM
        ),
        cost_estimate=pl.CostEstimate(
            flops=2 * weight * rows * count * (WIDTH + LATENT),
            bytes_accessed=weight * (2 * count * WIDTH + rows * 4096),
            transcendentals=weight * rows * count,
        ),
    )(*args)


def merge_kernel(own_ref, other_ref, out_ref):
    _, toks, width = own_ref.shape
    wide = width - 128
    lane = lax.broadcasted_iota(jnp.int32, (128, wide), 0)
    head = lax.broadcasted_iota(jnp.int32, (128, wide), 1) // 128
    spread = ((lane >= 3 * head) & (lane < 3 * head + 3)).astype(jnp.float32).astype(jnp.bfloat16)
    for side in range(2):
        refs = (own_ref, side), (other_ref, 1 - side)
        own, other = [
            jnp.dot(r[s, :, wide:], spread, preferred_element_type=jnp.float32) for r, s in refs
        ]
        top = jnp.maximum(own, other)
        own, other = jnp.exp2(own - top), jnp.exp2(other - top)
        own_part, other_part = [r[s, :, :wide].astype(jnp.float32) for r, s in refs]
        out_ref[side * toks : (side + 1) * toks, :] = (
            (own_part * own + other_part * other) * (1.0 / (own + other))
        ).astype(out_ref.dtype)


def merge(own, other):
    _, toks, width = own.shape
    return pl.pallas_call(
        merge_kernel,
        in_specs=[WHOLE] * 2,
        out_specs=WHOLE,
        out_shape=jax.ShapeDtypeStruct((2 * toks, width - 128), own.dtype),
        compiler_params=pltpu.CompilerParams(vmem_limit_bytes=VMEM),
    )(own, other)


def project_kernel(slots_ref, v_ref, w_ref, out_ref):
    near, core = slots_ref[0], slots_ref[1]
    toks = v_ref.shape[0] // 4
    for y in range(w_ref.shape[0]):
        part = lax.dot_general(v_ref[...], w_ref[y], NT, preferred_element_type=jnp.float32)
        part = part.astype(jnp.bfloat16)
        for k in range(4):
            at_near = near if k < 2 else 1 - near
            at_core = core if k % 2 == 0 else 1 - core
            out_ref[y % 4, at_near, at_core, y // 4] = part[k * toks : (k + 1) * toks]


def project(slots, v, w):
    blocks, cols, depth = w.shape
    toks = v.shape[0] // 4
    return pl.pallas_call(
        project_kernel,
        in_specs=[pl.BlockSpec(memory_space=pltpu.SMEM)] + [WHOLE] * 2,
        out_specs=WHOLE,
        out_shape=jax.ShapeDtypeStruct((4, 2, 2, blocks // 4, toks, cols), jnp.bfloat16),
        compiler_params=pltpu.CompilerParams(vmem_limit_bytes=VMEM),
        cost_estimate=pl.CostEstimate(
            flops=8 * toks * blocks * cols * depth,
            bytes_accessed=2 * blocks * cols * depth,
            transcendentals=0,
        ),
    )(slots, v, w)


def add_x_kernel(slots_ref, parts_ref, keep_ref, give_ref):
    here = slots_ref[2]
    for whose, out_ref in ((1 - here, give_ref), (here, keep_ref)):
        for near in range(2):
            total = []
            for core in range(2):
                t = parts_ref[0, near, core, whose].astype(jnp.float32)
                for x in range(1, parts_ref.shape[0]):
                    t += parts_ref[x, near, core, whose].astype(jnp.float32)
                total.append(t)
            for far in range(2):
                at = far * 256 + near * 128
                lanes = slice(far * 64, far * 64 + 64)
                out_ref[:, at : at + 128] = jnp.concatenate(
                    [t[:, lanes] for t in total], axis=1
                ).astype(out_ref.dtype)


def add_x(slots, parts):
    toks, cols = parts.shape[4:]
    return pl.pallas_call(
        add_x_kernel,
        in_specs=[pl.BlockSpec(memory_space=pltpu.SMEM), WHOLE],
        out_specs=[WHOLE] * 2,
        out_shape=[
            jax.ShapeDtypeStruct((toks, 4 * cols), jnp.float32),
            jax.ShapeDtypeStruct((toks, 4 * cols), parts.dtype),
        ],
        compiler_params=pltpu.CompilerParams(vmem_limit_bytes=VMEM),
    )(slots, parts)


def pair_kernel(far_ref, own_ref, other_ref, _, out_hbm, both_ref, sems):
    far = far_ref[0]
    both_ref[far] = own_ref[...]
    both_ref[1 - far] = other_ref[...]
    send_copies(both_ref, out_hbm, sems)


def pair(far, own, other, earlier, copies):
    corner = earlier.reshape(-1, earlier.shape[-1])[:16, :128]
    return pl.pallas_call(
        pair_kernel,
        in_specs=[pl.BlockSpec(memory_space=pltpu.SMEM)] + [WHOLE] * 3,
        out_specs=ANYWHERE,
        out_shape=jax.ShapeDtypeStruct((copies, 2) + own.shape, own.dtype),
        scratch_shapes=[
            pltpu.VMEM((2,) + own.shape, own.dtype),
            pltpu.SemaphoreType.DMA((copies,)),
        ],
        compiler_params=pltpu.CompilerParams(vmem_limit_bytes=VMEM),
    )(far, own, other, corner)


def on_device(queries, latents, positions, lengths, value_up, out_weight):
    toks, heads, width = queries.shape
    ends = jnp.cumsum(lengths).astype(jnp.int32)
    core = lax.axis_index("core").astype(jnp.int32)
    far = lax.axis_index("zh_lat").astype(jnp.int32)
    near = lax.axis_index("zl_lat").astype(jnp.int32)

    key_rows = prepare_keys(positions, latents, 8)
    along_y = lax.all_to_all(key_rows, "y", 0, 0).reshape(8 * toks, WIDTH)

    q_own = prepare_queries(positions, queries.transpose(1, 0, 2))
    q = jnp.concatenate([q_own, swap(q_own, "core")], axis=1)

    w = out_weight.T
    w = pair(far.reshape(1), w, swap(w, "zh_lat"), q, 8)
    w = lax.all_to_all(w, "y", 0, 0)
    w = w.reshape(8, -1, w.shape[3])

    next_own = shift_z(along_y)
    next_other = shift_z(swap(along_y, "core"))
    beyond = shift_z(next_own)
    carry = attend(ends, q, along_y, value_up, weight=3)
    carry = attend(ends, q, next_own, value_up, carry, weight=3)
    carry = attend(ends, q, next_other, value_up, carry, weight=3)
    part = attend(ends, q, beyond, value_up, carry, last=True)

    values = merge(part, swap(part, "core"))

    v = jnp.concatenate([values, swap(values, "zl_lat")], axis=0)

    z_hi = lax.axis_index("z_hi").astype(jnp.int32)
    slots = jnp.stack([near, core, z_hi])
    partial = project(slots, v, w)
    parts = lax.all_to_all(
        partial.reshape((16,) + partial.shape[3:]), ("x", "zl_lat", "core"), 0, 0
    )
    keep, give = add_x(slots, parts.reshape(partial.shape))
    return (keep + swap(give, "z_hi").astype(jnp.float32)).astype(jnp.bfloat16)


def solution(mesh):
    grid = Mesh(
        mesh.devices.reshape(8, 2, 2, 2, 2, 4), ("y", "zh_lat", "zl_lat", "core", "z_hi", "x")
    )
    seq, head = ("y", "zh_lat", "zl_lat", "core"), ("z_hi", "x")
    placed = (
        P(seq, head, None),
        P(seq, None),
        P(seq),
        P(),
        P(head, None, None),
        P(head, seq),
    )
    return jax.shard_map(
        on_device, mesh=grid, in_specs=placed, out_specs=P(seq, head), check_vma=False
    )
```

```python
import functools
import math

import jax
import jax.numpy as jnp
from jax import lax
from jax.experimental import pallas as pl
from jax.experimental.pallas import tpu as pltpu
from jax.sharding import Mesh, PartitionSpec as P

LATENT = 512
ROPE = 64
WIDTH = 640
SCALE = 192.0 ** (-0.5)
LOG2_SCALE = SCALE * math.log2(math.e)
HIDDEN = -1e30
VMEM = 48 * 1024 * 1024
NT = (((1,), (1,)), ((), ()))
WHOLE = pl.BlockSpec(memory_space=pltpu.VMEM)
ANYWHERE = pl.BlockSpec(memory_space=pl.ANY)


def turns(where_ref):
    toks = where_ref.shape[1]
    row = lax.broadcasted_iota(jnp.int32, (toks, toks), 0)
    column = lax.broadcasted_iota(jnp.int32, (toks, toks), 1)
    spread = jnp.broadcast_to(where_ref[...], (toks, toks))
    where = jnp.sum(jnp.where(row == column, spread, 0).astype(jnp.float32), axis=1, keepdims=True)
    lane = lax.broadcasted_iota(jnp.int32, (toks, ROPE), 1)
    pair = (lane % (ROPE // 2)).astype(jnp.float32)
    angles = where * jnp.exp(pair * (-2.0 * math.log(10000.0) / ROPE))
    sines = jnp.sin(angles)
    return where, jnp.cos(angles), jnp.where(lane < ROPE // 2, -sines, sines)


def turned(rotary, cosines, sines):
    half = ROPE // 2
    other = jnp.concatenate([rotary[:, half:], rotary[:, :half]], axis=1)
    return rotary * cosines + other * sines


def position_parts(where):
    high = jnp.floor(where * (1.0 / 64.0))
    return high, where - 64.0 * high


def key_kernel(
    where_hbm, latents_hbm, out_hbm, where_ref, latents_ref, rows_ref, last_ref, in_sems, out_sems
):
    arrivals = [
        pltpu.make_async_copy(where_hbm, where_ref, in_sems.at[0]),
        pltpu.make_async_copy(latents_hbm, latents_ref, in_sems.at[1]),
    ]
    for arrival in arrivals:
        arrival.start()
    arrivals[0].wait()
    where, cosines, sines = turns(where_ref)
    arrivals[1].wait()
    rows_ref[...] = latents_ref[:, :LATENT]
    copies = range(out_hbm.shape[0])
    plain = [
        pltpu.make_async_copy(
            rows_ref, out_hbm.at[i, :, pl.ds(0, LATENT)], out_sems.at[0, i]
        )
        for i in copies
    ]
    for copy in plain:
        copy.start()
    rotary = turned(latents_ref[:, LATENT:].astype(jnp.float32), cosines, sines)
    lane = lax.broadcasted_iota(jnp.int32, rotary.shape, 1)
    high, low = position_parts(where)
    tail = jnp.where(lane == 0, high, jnp.where(lane == 1, low, 0.0))
    last_ref[...] = jnp.concatenate([rotary, tail], axis=1).astype(jnp.bfloat16)
    rest = [
        pltpu.make_async_copy(last_ref, out_hbm.at[i, :, pl.ds(LATENT, 128)], out_sems.at[1, i])
        for i in copies
    ]
    for copy in rest:
        copy.start()
    for copy in plain + rest:
        copy.wait()


def send_copies(ref, out_hbm, sems):
    copies = [pltpu.make_async_copy(ref, out_hbm.at[i], sems.at[i]) for i in range(out_hbm.shape[0])]
    for copy in copies:
        copy.start()
    for copy in copies:
        copy.wait()


def prepare_keys(positions, latents, copies):
    toks, width = latents.shape
    return pl.pallas_call(
        key_kernel,
        in_specs=[pl.BlockSpec(memory_space=pltpu.HBM)] * 2,
        out_specs=ANYWHERE,
        out_shape=jax.ShapeDtypeStruct((copies, toks, WIDTH), latents.dtype),
        scratch_shapes=[
            pltpu.VMEM((1, toks), jnp.int32),
            pltpu.VMEM((toks, width), latents.dtype),
            pltpu.VMEM((toks, LATENT), latents.dtype),
            pltpu.VMEM((toks, WIDTH - LATENT), latents.dtype),
            pltpu.SemaphoreType.DMA((2,)),
            pltpu.SemaphoreType.DMA((2, copies)),
        ],
        compiler_params=pltpu.CompilerParams(vmem_limit_bytes=60 * 1024 * 1024),
    )(positions.reshape(1, -1), latents)


def query_kernel(where_ref, queries_ref, out_ref):
    where, cosines, sines = turns(where_ref)
    lane = lax.broadcasted_iota(jnp.int32, sines.shape, 1)
    high, low = position_parts(where)
    tail = jnp.where(lane == 2, high, jnp.where(lane == 3, low, 0.0))
    for h in range(queries_ref.shape[0]):
        rotary = turned(queries_ref[h, :, LATENT:].astype(jnp.float32), cosines, sines)
        out_ref[h, :, :LATENT] = queries_ref[h, :, :LATENT]
        out_ref[h, :, LATENT:] = jnp.concatenate([rotary, tail], axis=1).astype(jnp.bfloat16)


def prepare_queries(positions, queries):
    heads, toks, _ = queries.shape
    return pl.pallas_call(
        query_kernel,
        in_specs=[WHOLE] * 2,
        out_specs=WHOLE,
        out_shape=jax.ShapeDtypeStruct((heads, toks, WIDTH), queries.dtype),
        compiler_params=pltpu.CompilerParams(vmem_limit_bytes=VMEM),
    )(positions.reshape(1, -1), queries)


def shift_z(x):
    perm = []
    for z in range(8):
        for core in range(2):
            to = (z + 1 - 2 * core) % 8
            source = ((z % 4) * 2 + core) * 2 + z // 4
            target = ((to % 4) * 2 + core) * 2 + to // 4
            perm.append((source, target))
    return lax.ppermute(x, ("zh_lat", "zl_lat", "core", "z_hi"), perm)


def swap(x, axis):
    return lax.ppermute(x, axis, [(0, 1), (1, 0)])


def attend_kernel(group, first, last, ends_ref, q_ref, key_ref, up_ref, *refs):
    if first:
        key_hbm = key_ref
        top_out, total_out, part_out, key_ref, sem = refs
        arrival = pltpu.make_async_copy(key_hbm, key_ref, sem.at[0])
        arrival.start()
        arrival.wait()
    else:
        top_in, total_in, part_in = refs[:3]
        refs = refs[3:]
        if last:
            (out_ref,) = refs
        else:
            top_out, total_out, part_out = refs
    heads, toks, _ = q_ref.shape
    half = toks // 2
    meta = q_ref[0, :, LATENT:].astype(jnp.float32)
    query_pos = meta[:, 66:67] * 64.0 + meta[:, 67:68]
    query_start = jnp.zeros_like(query_pos)
    for k in range(8):
        end = ends_ref[k].astype(jnp.float32)
        query_start = jnp.where(query_pos >= end, end, query_start)
    first_end = ends_ref[0].astype(jnp.float32)
    lane = lax.broadcasted_iota(jnp.int32, (toks, 128), 1)
    pick = jnp.where(lane == 64, 64.0, jnp.where(lane == 65, 1.0, 0.0)).astype(jnp.bfloat16)
    key_pos = lax.dot_general(
        pick, key_ref[:, LATENT:], NT, preferred_element_type=jnp.float32
    )
    visible = (key_pos <= query_pos) & ((key_pos >= query_start) | (key_pos < first_end))
    count = key_ref.shape[0]
    rows = group * toks
    levels = jnp.zeros((toks, 128), jnp.float32)
    for at in range(0, heads, group):
        some = slice(at, at + group)
        raw = lax.dot_general(
            q_ref[some].reshape(rows, WIDTH), key_ref[...], NT, preferred_element_type=jnp.float32
        )
        raw = raw.reshape(group, toks, count)
        scores = jnp.where(visible[None], raw, HIDDEN).reshape(rows, count)
        wide = lambda column: jnp.broadcast_to(column, (rows, 128))
        top = wide(jnp.max(scores, axis=1, keepdims=True))
        if not first:
            old = top_in[some].reshape(rows, 128)
            top = jnp.maximum(top, old)
            fade = jnp.exp2((old - top) * LOG2_SCALE)
        weights = jnp.exp2((scores - jnp.concatenate([top] * (count // 128), axis=1)) * LOG2_SCALE)
        total = wide(jnp.sum(weights, axis=1, keepdims=True))
        if not first:
            total = total + fade * total_in[some].reshape(rows, 128)
        context = jnp.dot(
            weights.astype(jnp.bfloat16), key_ref[:, :LATENT], preferred_element_type=jnp.float32
        ).astype(jnp.bfloat16)
        if last:
            inverse = 1.0 / total
            level = top * LOG2_SCALE + jnp.log2(total)
            high = level.astype(jnp.bfloat16).astype(jnp.float32)
            middle = (level - high).astype(jnp.bfloat16).astype(jnp.float32)
            low = level - high - middle
        else:
            top_out[some] = top.reshape(group, toks, 128)
            total_out[some] = total.reshape(group, toks, 128)
        for h in range(group):
            mine = slice(h * toks, h * toks + toks)
            part = jnp.dot(context[mine], up_ref[at + h], preferred_element_type=jnp.float32)
            if not first:
                part = part + fade[mine] * part_in[at + h]
            if not last:
                part_out[at + h] = part
                continue
            part = (part * inverse[mine]).astype(jnp.bfloat16)
            lanes = slice((at + h) * 128, (at + h) * 128 + 128)
            for side in range(2):
                out_ref[side, :, lanes] = part[side * half : (side + 1) * half]
            for piece, value in enumerate((high, middle, low)):
                levels = jnp.where(lane == 3 * (at + h) + piece, value[mine], levels)
    if last:
        levels = levels.astype(jnp.bfloat16)
        for side in range(2):
            out_ref[side, :, heads * 128 :] = levels[side * half : (side + 1) * half]


def attend(ends, q, keys, up, carry=None, last=False, group=8, weight=1):
    heads, toks, _ = q.shape
    first = carry is None
    args = [ends, q, keys, up] + list(carry or ())
    if last:
        out_shape = jax.ShapeDtypeStruct((2, toks // 2, heads * 128 + 128), jnp.bfloat16)
    else:
        out_shape = [jax.ShapeDtypeStruct((heads, toks, 128), jnp.float32)] * 3
    rows, count = heads * toks, keys.shape[0]
    return pl.pallas_call(
        functools.partial(attend_kernel, group, first, last),
        in_specs=[
            pl.BlockSpec(memory_space=pltpu.SMEM),
            WHOLE,
            pl.BlockSpec(memory_space=pltpu.HBM) if first else WHOLE,
        ]
        + [WHOLE] * (len(args) - 3),
        out_specs=WHOLE if last else [WHOLE] * 3,
        out_shape=out_shape,
        scratch_shapes=[pltpu.VMEM(keys.shape, keys.dtype), pltpu.SemaphoreType.DMA((1,))]
        if first
        else [],
        compiler_params=pltpu.CompilerParams(
            vmem_limit_bytes=56 * 1024 * 1024 if first else VMEM
        ),
        cost_estimate=pl.CostEstimate(
            flops=2 * weight * rows * count * (WIDTH + LATENT),
            bytes_accessed=weight * (2 * count * WIDTH + rows * 4096),
            transcendentals=weight * rows * count,
        ),
    )(*args)


def merge_kernel(own_ref, other_ref, out_ref):
    _, toks, width = own_ref.shape
    wide = width - 128
    lane = lax.broadcasted_iota(jnp.int32, (128, wide), 0)
    head = lax.broadcasted_iota(jnp.int32, (128, wide), 1) // 128
    spread = ((lane >= 3 * head) & (lane < 3 * head + 3)).astype(jnp.float32).astype(jnp.bfloat16)
    for side in range(2):
        refs = (own_ref, side), (other_ref, 1 - side)
        own, other = [
            jnp.dot(r[s, :, wide:], spread, preferred_element_type=jnp.float32) for r, s in refs
        ]
        top = jnp.maximum(own, other)
        own, other = jnp.exp2(own - top), jnp.exp2(other - top)
        own_part, other_part = [r[s, :, :wide].astype(jnp.float32) for r, s in refs]
        out_ref[side * toks : (side + 1) * toks, :] = (
            (own_part * own + other_part * other) * (1.0 / (own + other))
        ).astype(out_ref.dtype)


def merge(own, other):
    _, toks, width = own.shape
    return pl.pallas_call(
        merge_kernel,
        in_specs=[WHOLE] * 2,
        out_specs=WHOLE,
        out_shape=jax.ShapeDtypeStruct((2 * toks, width - 128), own.dtype),
        compiler_params=pltpu.CompilerParams(vmem_limit_bytes=VMEM),
    )(own, other)


def project_kernel(slots_ref, v_ref, w_ref, out_ref):
    near, core = slots_ref[0], slots_ref[1]
    toks = v_ref.shape[0] // 4
    for y in range(w_ref.shape[0]):
        part = lax.dot_general(v_ref[...], w_ref[y], NT, preferred_element_type=jnp.float32)
        part = part.astype(jnp.bfloat16)
        for k in range(4):
            at_near = near if k < 2 else 1 - near
            at_core = core if k % 2 == 0 else 1 - core
            out_ref[y % 4, at_near, at_core, y // 4] = part[k * toks : (k + 1) * toks]


def project(slots, v, w):
    blocks, cols, depth = w.shape
    toks = v.shape[0] // 4
    return pl.pallas_call(
        project_kernel,
        in_specs=[pl.BlockSpec(memory_space=pltpu.SMEM)] + [WHOLE] * 2,
        out_specs=WHOLE,
        out_shape=jax.ShapeDtypeStruct((4, 2, 2, blocks // 4, toks, cols), jnp.bfloat16),
        compiler_params=pltpu.CompilerParams(vmem_limit_bytes=VMEM),
        cost_estimate=pl.CostEstimate(
            flops=8 * toks * blocks * cols * depth,
            bytes_accessed=2 * blocks * cols * depth,
            transcendentals=0,
        ),
    )(slots, v, w)


def add_x_kernel(slots_ref, parts_ref, keep_ref, give_ref):
    here = slots_ref[2]
    for whose, out_ref in ((1 - here, give_ref), (here, keep_ref)):
        for near in range(2):
            total = []
            for core in range(2):
                t = parts_ref[0, near, core, whose].astype(jnp.float32)
                for x in range(1, parts_ref.shape[0]):
                    t += parts_ref[x, near, core, whose].astype(jnp.float32)
                total.append(t)
            for far in range(2):
                at = far * 256 + near * 128
                lanes = slice(far * 64, far * 64 + 64)
                out_ref[:, at : at + 128] = jnp.concatenate(
                    [t[:, lanes] for t in total], axis=1
                ).astype(out_ref.dtype)


def add_x(slots, parts):
    toks, cols = parts.shape[4:]
    return pl.pallas_call(
        add_x_kernel,
        in_specs=[pl.BlockSpec(memory_space=pltpu.SMEM), WHOLE],
        out_specs=[WHOLE] * 2,
        out_shape=[
            jax.ShapeDtypeStruct((toks, 4 * cols), jnp.float32),
            jax.ShapeDtypeStruct((toks, 4 * cols), parts.dtype),
        ],
        compiler_params=pltpu.CompilerParams(vmem_limit_bytes=VMEM),
    )(slots, parts)


def pair_kernel(far_ref, own_ref, other_ref, _, out_hbm, both_ref, sems):
    far = far_ref[0]
    both_ref[far] = own_ref[...]
    both_ref[1 - far] = other_ref[...]
    send_copies(both_ref, out_hbm, sems)


def pair(far, own, other, earlier, copies):
    corner = earlier.reshape(-1, earlier.shape[-1])[:16, :128]
    return pl.pallas_call(
        pair_kernel,
        in_specs=[pl.BlockSpec(memory_space=pltpu.SMEM)] + [WHOLE] * 3,
        out_specs=ANYWHERE,
        out_shape=jax.ShapeDtypeStruct((copies, 2) + own.shape, own.dtype),
        scratch_shapes=[
            pltpu.VMEM((2,) + own.shape, own.dtype),
            pltpu.SemaphoreType.DMA((copies,)),
        ],
        compiler_params=pltpu.CompilerParams(vmem_limit_bytes=VMEM),
    )(far, own, other, corner)


def on_device(queries, latents, positions, lengths, value_up, out_weight):
    toks, heads, width = queries.shape
    ends = jnp.cumsum(lengths).astype(jnp.int32)
    core = lax.axis_index("core").astype(jnp.int32)
    far = lax.axis_index("zh_lat").astype(jnp.int32)
    near = lax.axis_index("zl_lat").astype(jnp.int32)

    key_rows = prepare_keys(positions, latents, 8)
    along_y = lax.all_to_all(key_rows, "y", 0, 0).reshape(8 * toks, WIDTH)

    q_own = prepare_queries(positions, queries.transpose(1, 0, 2))
    q = jnp.concatenate([q_own, swap(q_own, "core")], axis=1)

    w = out_weight.T
    w = pair(far.reshape(1), w, swap(w, "zh_lat"), q, 8)
    w = lax.all_to_all(w, "y", 0, 0)
    w = w.reshape(8, -1, w.shape[3])

    next_own = shift_z(along_y)
    next_other = shift_z(swap(along_y, "core"))
    beyond = shift_z(next_own)
    carry = attend(ends, q, along_y, value_up, weight=3)
    carry = attend(ends, q, next_own, value_up, carry, weight=3)
    carry = attend(ends, q, next_other, value_up, carry, weight=3)
    part = attend(ends, q, beyond, value_up, carry, last=True)

    values = merge(part, swap(part, "core"))

    v = jnp.concatenate([values, swap(values, "zl_lat")], axis=0)

    z_hi = lax.axis_index("z_hi").astype(jnp.int32)
    slots = jnp.stack([near, core, z_hi])
    partial = project(slots, v, w)
    parts = lax.all_to_all(
        partial.reshape((16,) + partial.shape[3:]), ("x", "zl_lat", "core"), 0, 0
    )
    keep, give = add_x(slots, parts.reshape(partial.shape))
    return (keep + swap(give, "z_hi").astype(jnp.float32)).astype(jnp.bfloat16)


def solution(mesh):
    grid = Mesh(
        mesh.devices.reshape(8, 2, 2, 2, 2, 4), ("y", "zh_lat", "zl_lat", "core", "z_hi", "x")
    )
    seq, head = ("y", "zh_lat", "zl_lat", "core"), ("z_hi", "x")
    placed = (
        P(seq, head, None),
        P(seq, None),
        P(seq),
        P(),
        P(head, None, None),
        P(head, seq),
    )
    return jax.shard_map(
        on_device, mesh=grid, in_specs=placed, out_specs=P(seq, head), check_vma=False
    )
```

```python
import functools
import math

import jax
import jax.numpy as jnp
from jax import lax
from jax.experimental import pallas as pl
from jax.experimental.pallas import tpu as pltpu
from jax.sharding import Mesh, PartitionSpec as P

LATENT = 512
ROPE = 64
WIDTH = 640
SCALE = 192.0 ** (-0.5)
LOG2_SCALE = SCALE * math.log2(math.e)
HIDDEN = -1e30
VMEM = 48 * 1024 * 1024
NT = (((1,), (1,)), ((), ()))
WHOLE = pl.BlockSpec(memory_space=pltpu.VMEM)
ANYWHERE = pl.BlockSpec(memory_space=pl.ANY)


def turns(where_ref):
    toks = where_ref.shape[1]
    row = lax.broadcasted_iota(jnp.int32, (toks, toks), 0)
    column = lax.broadcasted_iota(jnp.int32, (toks, toks), 1)
    spread = jnp.broadcast_to(where_ref[...], (toks, toks))
    where = jnp.sum(jnp.where(row == column, spread, 0).astype(jnp.float32), axis=1, keepdims=True)
    lane = lax.broadcasted_iota(jnp.int32, (toks, ROPE), 1)
    pair = (lane % (ROPE // 2)).astype(jnp.float32)
    angles = where * jnp.exp(pair * (-2.0 * math.log(10000.0) / ROPE))
    sines = jnp.sin(angles)
    return where, jnp.cos(angles), jnp.where(lane < ROPE // 2, -sines, sines)


def turned(rotary, cosines, sines):
    half = ROPE // 2
    other = jnp.concatenate([rotary[:, half:], rotary[:, :half]], axis=1)
    return rotary * cosines + other * sines


def position_parts(where):
    high = jnp.floor(where * (1.0 / 64.0))
    return high, where - 64.0 * high


def key_kernel(
    where_hbm, latents_hbm, out_hbm, where_ref, latents_ref, rows_ref, last_ref, in_sems, out_sems
):
    arrivals = [
        pltpu.make_async_copy(where_hbm, where_ref, in_sems.at[0]),
        pltpu.make_async_copy(latents_hbm, latents_ref, in_sems.at[1]),
    ]
    for arrival in arrivals:
        arrival.start()
    arrivals[0].wait()
    where, cosines, sines = turns(where_ref)
    arrivals[1].wait()
    rows_ref[...] = latents_ref[:, :LATENT]
    copies = range(out_hbm.shape[0])
    plain = [
        pltpu.make_async_copy(
            rows_ref, out_hbm.at[i, :, pl.ds(0, LATENT)], out_sems.at[0, i]
        )
        for i in copies
    ]
    for copy in plain:
        copy.start()
    rotary = turned(latents_ref[:, LATENT:].astype(jnp.float32), cosines, sines)
    lane = lax.broadcasted_iota(jnp.int32, rotary.shape, 1)
    high, low = position_parts(where)
    tail = jnp.where(lane == 0, high, jnp.where(lane == 1, low, 0.0))
    last_ref[...] = jnp.concatenate([rotary, tail], axis=1).astype(jnp.bfloat16)
    rest = [
        pltpu.make_async_copy(last_ref, out_hbm.at[i, :, pl.ds(LATENT, 128)], out_sems.at[1, i])
        for i in copies
    ]
    for copy in rest:
        copy.start()
    for copy in plain + rest:
        copy.wait()


def send_copies(ref, out_hbm, sems):
    copies = [pltpu.make_async_copy(ref, out_hbm.at[i], sems.at[i]) for i in range(out_hbm.shape[0])]
    for copy in copies:
        copy.start()
    for copy in copies:
        copy.wait()


def prepare_keys(positions, latents, copies):
    toks, width = latents.shape
    return pl.pallas_call(
        key_kernel,
        in_specs=[pl.BlockSpec(memory_space=pltpu.HBM)] * 2,
        out_specs=ANYWHERE,
        out_shape=jax.ShapeDtypeStruct((copies, toks, WIDTH), latents.dtype),
        scratch_shapes=[
            pltpu.VMEM((1, toks), jnp.int32),
            pltpu.VMEM((toks, width), latents.dtype),
            pltpu.VMEM((toks, LATENT), latents.dtype),
            pltpu.VMEM((toks, WIDTH - LATENT), latents.dtype),
            pltpu.SemaphoreType.DMA((2,)),
            pltpu.SemaphoreType.DMA((2, copies)),
        ],
        compiler_params=pltpu.CompilerParams(vmem_limit_bytes=60 * 1024 * 1024),
    )(positions.reshape(1, -1), latents)


def query_kernel(where_ref, queries_ref, out_ref):
    where, cosines, sines = turns(where_ref)
    lane = lax.broadcasted_iota(jnp.int32, sines.shape, 1)
    high, low = position_parts(where)
    tail = jnp.where(lane == 2, high, jnp.where(lane == 3, low, 0.0))
    for h in range(queries_ref.shape[0]):
        rotary = turned(queries_ref[h, :, LATENT:].astype(jnp.float32), cosines, sines)
        out_ref[h, :, :LATENT] = queries_ref[h, :, :LATENT]
        out_ref[h, :, LATENT:] = jnp.concatenate([rotary, tail], axis=1).astype(jnp.bfloat16)


def prepare_queries(positions, queries):
    heads, toks, _ = queries.shape
    return pl.pallas_call(
        query_kernel,
        in_specs=[WHOLE] * 2,
        out_specs=WHOLE,
        out_shape=jax.ShapeDtypeStruct((heads, toks, WIDTH), queries.dtype),
        compiler_params=pltpu.CompilerParams(vmem_limit_bytes=VMEM),
    )(positions.reshape(1, -1), queries)


def shift_z(x):
    perm = []
    for z in range(8):
        for core in range(2):
            to = (z + 1 - 2 * core) % 8
            source = ((z % 4) * 2 + core) * 2 + z // 4
            target = ((to % 4) * 2 + core) * 2 + to // 4
            perm.append((source, target))
    return lax.ppermute(x, ("zh_lat", "zl_lat", "core", "z_hi"), perm)


def swap(x, axis):
    return lax.ppermute(x, axis, [(0, 1), (1, 0)])


def attend_kernel(group, first, last, ends_ref, q_ref, key_ref, up_ref, *refs):
    if first:
        key_hbm = key_ref
        top_out, total_out, part_out, key_ref, sem = refs
        arrival = pltpu.make_async_copy(key_hbm, key_ref, sem.at[0])
        arrival.start()
        arrival.wait()
    else:
        top_in, total_in, part_in = refs[:3]
        refs = refs[3:]
        if last:
            (out_ref,) = refs
        else:
            top_out, total_out, part_out = refs
    heads, toks, _ = q_ref.shape
    half = toks // 2
    meta = q_ref[0, :, LATENT:].astype(jnp.float32)
    query_pos = meta[:, 66:67] * 64.0 + meta[:, 67:68]
    query_start = jnp.zeros_like(query_pos)
    for k in range(8):
        end = ends_ref[k].astype(jnp.float32)
        query_start = jnp.where(query_pos >= end, end, query_start)
    first_end = ends_ref[0].astype(jnp.float32)
    lane = lax.broadcasted_iota(jnp.int32, (toks, 128), 1)
    pick = jnp.where(lane == 64, 64.0, jnp.where(lane == 65, 1.0, 0.0)).astype(jnp.bfloat16)
    key_pos = lax.dot_general(
        pick, key_ref[:, LATENT:], NT, preferred_element_type=jnp.float32
    )
    visible = (key_pos <= query_pos) & ((key_pos >= query_start) | (key_pos < first_end))
    count = key_ref.shape[0]
    rows = group * toks
    levels = jnp.zeros((toks, 128), jnp.float32)
    for at in range(0, heads, group):
        some = slice(at, at + group)
        raw = lax.dot_general(
            q_ref[some].reshape(rows, WIDTH), key_ref[...], NT, preferred_element_type=jnp.float32
        )
        raw = raw.reshape(group, toks, count)
        scores = jnp.where(visible[None], raw, HIDDEN).reshape(rows, count)
        wide = lambda column: jnp.broadcast_to(column, (rows, 128))
        top = wide(jnp.max(scores, axis=1, keepdims=True))
        if not first:
            old = top_in[some].reshape(rows, 128)
            top = jnp.maximum(top, old)
            fade = jnp.exp2((old - top) * LOG2_SCALE)
        weights = jnp.exp2((scores - jnp.concatenate([top] * (count // 128), axis=1)) * LOG2_SCALE)
        total = wide(jnp.sum(weights, axis=1, keepdims=True))
        if not first:
            total = total + fade * total_in[some].reshape(rows, 128)
        context = jnp.dot(
            weights.astype(jnp.bfloat16), key_ref[:, :LATENT], preferred_element_type=jnp.float32
        ).astype(jnp.bfloat16)
        if last:
            inverse = 1.0 / total
            level = top * LOG2_SCALE + jnp.log2(total)
            high = level.astype(jnp.bfloat16).astype(jnp.float32)
            middle = (level - high).astype(jnp.bfloat16).astype(jnp.float32)
            low = level - high - middle
        else:
            top_out[some] = top.reshape(group, toks, 128)
            total_out[some] = total.reshape(group, toks, 128)
        for h in range(group):
            mine = slice(h * toks, h * toks + toks)
            part = jnp.dot(context[mine], up_ref[at + h], preferred_element_type=jnp.float32)
            if not first:
                part = part + fade[mine] * part_in[at + h]
            if not last:
                part_out[at + h] = part
                continue
            part = (part * inverse[mine]).astype(jnp.bfloat16)
            lanes = slice((at + h) * 128, (at + h) * 128 + 128)
            for side in range(2):
                out_ref[side, :, lanes] = part[side * half : (side + 1) * half]
            for piece, value in enumerate((high, middle, low)):
                levels = jnp.where(lane == 3 * (at + h) + piece, value[mine], levels)
    if last:
        levels = levels.astype(jnp.bfloat16)
        for side in range(2):
            out_ref[side, :, heads * 128 :] = levels[side * half : (side + 1) * half]


def attend(ends, q, keys, up, carry=None, last=False, group=8, weight=1):
    heads, toks, _ = q.shape
    first = carry is None
    args = [ends, q, keys, up] + list(carry or ())
    if last:
        out_shape = jax.ShapeDtypeStruct((2, toks // 2, heads * 128 + 128), jnp.bfloat16)
    else:
        out_shape = [jax.ShapeDtypeStruct((heads, toks, 128), jnp.float32)] * 3
    rows, count = heads * toks, keys.shape[0]
    return pl.pallas_call(
        functools.partial(attend_kernel, group, first, last),
        in_specs=[
            pl.BlockSpec(memory_space=pltpu.SMEM),
            WHOLE,
            pl.BlockSpec(memory_space=pltpu.HBM) if first else WHOLE,
        ]
        + [WHOLE] * (len(args) - 3),
        out_specs=WHOLE if last else [WHOLE] * 3,
        out_shape=out_shape,
        scratch_shapes=[pltpu.VMEM(keys.shape, keys.dtype), pltpu.SemaphoreType.DMA((1,))]
        if first
        else [],
        compiler_params=pltpu.CompilerParams(
            vmem_limit_bytes=56 * 1024 * 1024 if first else VMEM
        ),
        cost_estimate=pl.CostEstimate(
            flops=2 * weight * rows * count * (WIDTH + LATENT),
            bytes_accessed=weight * (2 * count * WIDTH + rows * 4096),
            transcendentals=weight * rows * count,
        ),
    )(*args)


def merge_kernel(own_ref, other_ref, out_ref):
    _, toks, width = own_ref.shape
    wide = width - 128
    lane = lax.broadcasted_iota(jnp.int32, (128, wide), 0)
    head = lax.broadcasted_iota(jnp.int32, (128, wide), 1) // 128
    spread = ((lane >= 3 * head) & (lane < 3 * head + 3)).astype(jnp.float32).astype(jnp.bfloat16)
    for side in range(2):
        refs = (own_ref, side), (other_ref, 1 - side)
        own, other = [
            jnp.dot(r[s, :, wide:], spread, preferred_element_type=jnp.float32) for r, s in refs
        ]
        top = jnp.maximum(own, other)
        own, other = jnp.exp2(own - top), jnp.exp2(other - top)
        own_part, other_part = [r[s, :, :wide].astype(jnp.float32) for r, s in refs]
        out_ref[side * toks : (side + 1) * toks, :] = (
            (own_part * own + other_part * other) * (1.0 / (own + other))
        ).astype(out_ref.dtype)


def merge(own, other):
    _, toks, width = own.shape
    return pl.pallas_call(
        merge_kernel,
        in_specs=[WHOLE] * 2,
        out_specs=WHOLE,
        out_shape=jax.ShapeDtypeStruct((2 * toks, width - 128), own.dtype),
        compiler_params=pltpu.CompilerParams(vmem_limit_bytes=VMEM),
    )(own, other)


def project_kernel(slots_ref, v_ref, w_ref, out_ref):
    near, core = slots_ref[0], slots_ref[1]
    toks = v_ref.shape[0] // 4
    for y in range(w_ref.shape[0]):
        part = lax.dot_general(v_ref[...], w_ref[y], NT, preferred_element_type=jnp.float32)
        part = part.astype(jnp.bfloat16)
        for k in range(4):
            at_near = near if k < 2 else 1 - near
            at_core = core if k % 2 == 0 else 1 - core
            out_ref[y % 4, at_near, at_core, y // 4] = part[k * toks : (k + 1) * toks]


def project(slots, v, w):
    blocks, cols, depth = w.shape
    toks = v.shape[0] // 4
    return pl.pallas_call(
        project_kernel,
        in_specs=[pl.BlockSpec(memory_space=pltpu.SMEM)] + [WHOLE] * 2,
        out_specs=WHOLE,
        out_shape=jax.ShapeDtypeStruct((4, 2, 2, blocks // 4, toks, cols), jnp.bfloat16),
        compiler_params=pltpu.CompilerParams(vmem_limit_bytes=VMEM),
        cost_estimate=pl.CostEstimate(
            flops=8 * toks * blocks * cols * depth,
            bytes_accessed=2 * blocks * cols * depth,
            transcendentals=0,
        ),
    )(slots, v, w)


def add_x_kernel(slots_ref, parts_ref, keep_ref, give_ref):
    here = slots_ref[2]
    for whose, out_ref in ((1 - here, give_ref), (here, keep_ref)):
        for near in range(2):
            total = []
            for core in range(2):
                t = parts_ref[0, near, core, whose].astype(jnp.float32)
                for x in range(1, parts_ref.shape[0]):
                    t += parts_ref[x, near, core, whose].astype(jnp.float32)
                total.append(t)
            for far in range(2):
                at = far * 256 + near * 128
                lanes = slice(far * 64, far * 64 + 64)
                out_ref[:, at : at + 128] = jnp.concatenate(
                    [t[:, lanes] for t in total], axis=1
                ).astype(out_ref.dtype)


def add_x(slots, parts):
    toks, cols = parts.shape[4:]
    return pl.pallas_call(
        add_x_kernel,
        in_specs=[pl.BlockSpec(memory_space=pltpu.SMEM), WHOLE],
        out_specs=[WHOLE] * 2,
        out_shape=[
            jax.ShapeDtypeStruct((toks, 4 * cols), jnp.float32),
            jax.ShapeDtypeStruct((toks, 4 * cols), parts.dtype),
        ],
        compiler_params=pltpu.CompilerParams(vmem_limit_bytes=VMEM),
    )(slots, parts)


def add_z_kernel(keep_ref, arrived_ref, out_ref):
    total = keep_ref[...] + arrived_ref[...].astype(jnp.float32)
    out_ref[...] = total.astype(out_ref.dtype)


def add_z(keep, arrived):
    return pl.pallas_call(
        add_z_kernel,
        in_specs=[WHOLE] * 2,
        out_specs=WHOLE,
        out_shape=jax.ShapeDtypeStruct(arrived.shape, arrived.dtype),
        compiler_params=pltpu.CompilerParams(vmem_limit_bytes=VMEM),
    )(keep, arrived)


def pair_kernel(far_ref, own_ref, other_ref, _, out_hbm, both_ref, sems):
    far = far_ref[0]
    both_ref[far] = own_ref[...]
    both_ref[1 - far] = other_ref[...]
    send_copies(both_ref, out_hbm, sems)


def pair(far, own, other, earlier, copies):
    corner = earlier.reshape(-1, earlier.shape[-1])[:16, :128]
    return pl.pallas_call(
        pair_kernel,
        in_specs=[pl.BlockSpec(memory_space=pltpu.SMEM)] + [WHOLE] * 3,
        out_specs=ANYWHERE,
        out_shape=jax.ShapeDtypeStruct((copies, 2) + own.shape, own.dtype),
        scratch_shapes=[
            pltpu.VMEM((2,) + own.shape, own.dtype),
            pltpu.SemaphoreType.DMA((copies,)),
        ],
        compiler_params=pltpu.CompilerParams(vmem_limit_bytes=VMEM),
    )(far, own, other, corner)


def on_device(queries, latents, positions, lengths, value_up, out_weight):
    toks, heads, width = queries.shape
    ends = jnp.cumsum(lengths).astype(jnp.int32)
    core = lax.axis_index("core").astype(jnp.int32)
    far = lax.axis_index("zh_lat").astype(jnp.int32)
    near = lax.axis_index("zl_lat").astype(jnp.int32)

    key_rows = prepare_keys(positions, latents, 8)
    along_y = lax.all_to_all(key_rows, "y", 0, 0).reshape(8 * toks, WIDTH)

    q_own = prepare_queries(positions, queries.transpose(1, 0, 2))
    q = jnp.concatenate([q_own, swap(q_own, "core")], axis=1)

    w = out_weight.T
    w = pair(far.reshape(1), w, swap(w, "zh_lat"), q, 8)
    w = lax.all_to_all(w, "y", 0, 0)
    w = w.reshape(8, -1, w.shape[3])

    next_own = shift_z(along_y)
    next_other = shift_z(swap(along_y, "core"))
    beyond = shift_z(next_own)
    carry = attend(ends, q, along_y, value_up, weight=3)
    carry = attend(ends, q, next_own, value_up, carry, weight=3)
    carry = attend(ends, q, next_other, value_up, carry, weight=3)
    part = attend(ends, q, beyond, value_up, carry, last=True)

    values = merge(part, swap(part, "core"))

    v = jnp.concatenate([values, swap(values, "zl_lat")], axis=0)

    z_hi = lax.axis_index("z_hi").astype(jnp.int32)
    slots = jnp.stack([near, core, z_hi])
    partial = project(slots, v, w)
    parts = lax.all_to_all(
        partial.reshape((16,) + partial.shape[3:]), ("x", "zl_lat", "core"), 0, 0
    )
    keep, give = add_x(slots, parts.reshape(partial.shape))
    return add_z(keep, swap(give, "z_hi"))


def solution(mesh):
    grid = Mesh(
        mesh.devices.reshape(8, 2, 2, 2, 2, 4), ("y", "zh_lat", "zl_lat", "core", "z_hi", "x")
    )
    seq, head = ("y", "zh_lat", "zl_lat", "core"), ("z_hi", "x")
    placed = (
        P(seq, head, None),
        P(seq, None),
        P(seq),
        P(),
        P(head, None, None),
        P(head, seq),
    )
    return jax.shard_map(
        on_device, mesh=grid, in_specs=placed, out_specs=P(seq, head), check_vma=False
    )
```
